32 devices in a mesh: slab: 16 (over z, x, core), col: 2 (over y).
Axes of the slice: x: 2, y: 2, z: 4, core: 2. Of those that a mesh axis runs over, the one named last changes fastest.
Arguments:
- density: float32 [32, 64, 256], P('slab', 'col'), may hold values from 0.5 to 2
- velocity: float32 [3, 32, 64, 256], P(None, 'slab', 'col'), may hold values from -3 to 3
- pressure: float32 [32, 64, 256], P('slab', 'col'), may hold values from 0.5 to 2
- fraction_code: int32 [32, 64, 256], P('slab', 'col'), may hold values from 8 to 16
- interface_cell: int32 [16, 2, 512], P('slab', 'col'), may hold values from 0 to 16383
- interface_element: int32 [16, 2, 512], P('slab', 'col'), may hold values from 0 to 255
- interface_count: int32 [16, 2], P('slab', 'col'), may hold values from 64 to 512, as said below
- wall_normal: float32 [3, 16, 2, 512], P(None, 'slab', 'col'), may hold values from -4 to 4
- element_mass: float32 [16, 256], P('slab'), may hold values from 0.5 to 2
- element_removed: int32 [16, 256], P('slab'), may hold values 0 or 1
- element_velocity: float32 [3, 16, 256], P(None, 'slab'), may hold values from -3 to 3
Outputs:
- new_state: float32 [5, 32, 64, 256], P(None, 'slab', 'col')
- new_velocity: float32 [3, 16, 256], P(None, 'slab', 'col')
The draws below stay inside these ranges and needn't reach their ends.
Inputs may be any that keep to these rules, and one draw needn't show every extreme that they name: `interface_cell`: index within the block of 2 x 32 x 256 cells of its slab and column. `interface_element`: element of the row's own slab group. `interface_count`: each count is 512, 256, 128 or 64; some slab and column has 512.
All inputs are finite; a program needn't handle non-finite values. No bound on the sum of `element_removed` on one device may be relied on, other than what follows from the above.
Results may differ from the reference program's by a relative error of at most 0.0003.
Values sent between devices are 32-bit elements; how exact they have to be, the bound alone decides.
A program may use at most 64 MiB of HBM per device.

```python
import math
import jax
import jax.numpy as jnp
from jax import lax

CX = 2
CY = 32
CZ = 256
I_DEV = 512
SLABS = 16
COLS = 2
NX = 32
NY = 64
E_GRP = 256


def draw_interface_count(key, part):
    key_one, key_two = jax.random.split(key)
    levels = jax.random.randint(key_one, (SLABS, COLS), 0, 4)
    counts = I_DEV // jnp.left_shift(jnp.ones_like(levels), levels)
    chosen_spot = jax.random.randint(key_two, (), 0, SLABS * COLS)
    flattened = counts.reshape(-1).at[chosen_spot].set(I_DEV)
    return flattened.reshape(SLABS, COLS).astype(jnp.int32)


def place_ends(drawn, rng, least, largest):
    place = [jax.random.randint(jax.random.fold_in(rng, axis), (), 0, length) for axis, length in enumerate(drawn.shape)]
    longest = drawn.shape.index(max(drawn.shape))
    neighbour = place[:longest] + [(place[longest] + 1) % drawn.shape[longest]] + place[longest + 1:]
    return drawn.at[tuple(place)].set(least).at[tuple(neighbour)].set(largest)


def block_scale(key, shape, shards, least, high):
    factor_of, own = 1.0, jax.random.fold_in(key, 6)
    for dim, parts in shards:
        heights = jnp.exp(jax.random.uniform(jax.random.fold_in(own, dim), (parts,), jnp.float32, least / len(shards), high / len(shards)))
        factor_of = factor_of * jnp.repeat(heights, shape[dim] // parts).reshape([-1 if axis == dim else 1 for axis in range(len(shape))])
    return factor_of


def centred(own_key, shape, deviation, most, pieces=(), held_as=jnp.bfloat16):
    gain = block_scale(own_key, shape, pieces, -0.22, 0.18) if pieces else 1.0
    values = jax.random.normal(own_key, shape, jnp.float32) * deviation * gain
    return jnp.minimum(jnp.maximum(values, -most), most).astype(held_as)


def setup_inputs(seed: int = 0) -> dict:
    arg_keys = jax.random.split(jax.random.key(seed), 12)
    density = jnp.clip(jnp.exp(math.log(2.0) - 1.3862944 * jax.random.uniform(arg_keys[0], (NX, NY, CZ), jnp.float32) ** block_scale(arg_keys[0], (NX, NY, CZ), ((0, 16), (1, 2)), -0.2, 0.2)), 0.5, 2.0)
    velocity = centred(arg_keys[1], (3, NX, NY, CZ), 0.5, 3.0, ((1, 16), (2, 2)), jnp.float32)
    pressure = jnp.clip(jnp.exp(math.log(2.0) - 1.3862944 * jax.random.uniform(arg_keys[2], (NX, NY, CZ), jnp.float32) ** block_scale(arg_keys[2], (NX, NY, CZ), ((0, 16), (1, 2)), -0.2, 0.2)), 0.5, 2.0)
    fraction_code = place_ends(jax.random.randint(arg_keys[3], (NX, NY, CZ), 8, 17), jax.random.fold_in(arg_keys[3], 1), 8, 16).astype(jnp.int32)
    interface_cell = place_ends(jax.random.randint(arg_keys[4], (SLABS, COLS, I_DEV), 0, CX * CY * CZ), jax.random.fold_in(arg_keys[4], 1), 0, (CX * CY * CZ) - 1).astype(jnp.int32)
    interface_element = place_ends(jax.random.randint(arg_keys[5], (SLABS, COLS, I_DEV), 0, E_GRP), jax.random.fold_in(arg_keys[5], 1), 0, E_GRP - 1).astype(jnp.int32)
    interface_count = draw_interface_count(jax.random.fold_in(arg_keys[11], 71), 0)
    wall_normal = centred(arg_keys[7], (3, SLABS, COLS, I_DEV), 1.0, 4.0, ((1, 16), (2, 2)), jnp.float32)
    element_mass = jnp.clip(jnp.exp(math.log(2.0) - 1.3862944 * jax.random.uniform(arg_keys[8], (SLABS, E_GRP), jnp.float32) ** block_scale(arg_keys[8], (SLABS, E_GRP), ((0, 16),), -0.2, 0.2)), 0.5, 2.0)
    element_removed = place_ends((jax.random.randint(arg_keys[9], (SLABS, E_GRP), 0, 4) < 1).astype(jnp.int32), jax.random.fold_in(arg_keys[9], 1), 0, 1)
    element_velocity = centred(arg_keys[10], (3, SLABS, E_GRP), 0.5, 3.0, ((1, 16),), jnp.float32)
    return {"density": density, "velocity": velocity, "pressure": pressure, "fraction_code": fraction_code, "interface_cell": interface_cell, "interface_element": interface_element, "interface_count": interface_count, "wall_normal": wall_normal, "element_mass": element_mass, "element_removed": element_removed, "element_velocity": element_velocity}


ratio_heat = 1.4
step_ratio = 0.1
struct_step = 1.0

def cell_terms(density_s, velocity_s, pressure_s, along):
    normal = velocity_s[along]
    energy = pressure_s / (ratio_heat - 1.0) + 0.5 * density_s * (velocity_s[0] * velocity_s[0] + velocity_s[1] * velocity_s[1] + velocity_s[2] * velocity_s[2])
    conserved = jnp.stack([density_s, density_s * velocity_s[0], density_s * velocity_s[1], density_s * velocity_s[2], energy])
    zero_plane = jnp.zeros_like(pressure_s)
    pressure_terms = [zero_plane, zero_plane, zero_plane, zero_plane, pressure_s * normal]
    pressure_terms[1 + along] = pressure_s
    flux_terms = normal[None] * conserved + jnp.stack(pressure_terms)
    wave_speed = jnp.abs(normal) + jnp.sqrt(ratio_heat * pressure_s / density_s)
    return (conserved, flux_terms, wave_speed)

def cut_range(array, start, stop, along):
    return lax.slice_in_dim(array, start, stop, axis=array.ndim - 3 + along)

def face_sum(conserved, flux_terms, wave_speed, fraction, along):
    extent = fraction.shape[along]

    def take_low(array):
        return cut_range(array, 0, extent - 1, along)

    def take_high(array):
        return cut_range(array, 1, extent, along)
    face_flux = 0.5 * (take_low(flux_terms) + take_high(flux_terms)) - 0.5 * jnp.maximum(take_low(wave_speed), take_high(wave_speed))[None] * (take_high(conserved) - take_low(conserved))
    weighted = jnp.minimum(take_low(fraction), take_high(fraction))[None] * face_flux
    return cut_range(weighted, 1, extent - 1, along) - cut_range(weighted, 0, extent - 2, along)

def interior(array, along):
    for other in range(3):
        if other != along:
            array = cut_range(array, 1, array.shape[array.ndim - 3 + other] - 1, other)
    return array

def divergence(density_p, velocity_p, pressure_p, fraction_p):
    live = fraction_p > 0.0
    density_s = jnp.where(live, density_p, 1.0)
    pressure_s = jnp.where(live, pressure_p, 1.0)
    summed = 0.0
    for along in range(3):
        conserved, flux_terms, wave_speed = cell_terms(interior(density_s, along), interior(velocity_p, along), interior(pressure_s, along), along)
        summed = summed + face_sum(conserved, flux_terms, wave_speed, interior(fraction_p, along), along)
    return summed

def reference(density, velocity, pressure, fraction_code, interface_cell, interface_element, interface_count, wall_normal, element_mass, element_removed, element_velocity):
    fraction = fraction_code.astype(jnp.float32) / 16.0
    slab_ids = jnp.arange(SLABS, dtype=jnp.int32)[:, None, None]
    column_ids = jnp.arange(COLS, dtype=jnp.int32)[None, :, None]
    plane_x = slab_ids * CX + interface_cell // (CY * CZ)
    plane_y = column_ids * CY + interface_cell // CZ % CY
    plane_z = interface_cell % CZ
    row_pressure = pressure[plane_x, plane_y, plane_z]
    row_fraction = fraction[plane_x, plane_y, plane_z]
    active = (jnp.arange(I_DEV, dtype=jnp.int32)[None, None, :] < interface_count[:, :, None]).astype(jnp.float32)
    weight = row_pressure * (1.0 - row_fraction) * active
    wall_force = -weight[None] * wall_normal
    segment_ids = (interface_element + slab_ids * E_GRP).reshape(-1)
    elem_loads = jax.ops.segment_sum(wall_force.reshape(3, -1).T, segment_ids, num_segments=SLABS * E_GRP).T.reshape(3, SLABS, E_GRP)
    keep_factor = 1.0 - element_removed.astype(jnp.float32)
    new_velocity = (element_velocity + struct_step * elem_loads / element_mass[None]) * keep_factor[None]
    row_motion = new_velocity[:, slab_ids, interface_element]
    wall_work = weight * lax.optimization_barrier(jnp.sum(wall_normal * row_motion, axis=0))
    row_terms = jnp.concatenate([weight[None] * wall_normal, wall_work[None]], axis=0)
    local_flat = interface_cell // (CY * CZ) * (NY * CZ) + plane_y * CZ + plane_z

    def one_slab(slab_pos):
        planes = slab_pos * CX - 1 + jnp.arange(CX + 2, dtype=jnp.int32)
        inside = (planes >= 0) & (planes < NX)
        clipped = jnp.clip(planes, 0, NX - 1)
        edge_pad = ((0, 0), (1, 1), (1, 1))
        fraction_p = jnp.pad(jnp.where(inside[:, None, None], jnp.take(fraction, clipped, axis=0), 0.0), edge_pad)
        density_p = jnp.pad(jnp.take(density, clipped, axis=0), edge_pad)
        pressure_p = jnp.pad(jnp.take(pressure, clipped, axis=0), edge_pad)
        velocity_p = jnp.pad(jnp.take(velocity, clipped, axis=1), ((0, 0),) + edge_pad)
        summed = divergence(density_p, velocity_p, pressure_p, fraction_p)
        centre = cell_terms(density_p[1:-1, 1:-1, 1:-1], velocity_p[:, 1:-1, 1:-1, 1:-1], pressure_p[1:-1, 1:-1, 1:-1], 0)[0]
        slab_rows = lax.dynamic_index_in_dim(row_terms, slab_pos, axis=1, keepdims=False).reshape(4, -1)
        slab_cells = lax.dynamic_index_in_dim(local_flat, slab_pos, axis=0, keepdims=False).reshape(-1)
        source = jnp.zeros((4, CX * NY * CZ), jnp.float32).at[:, slab_cells].add(slab_rows)
        source = jnp.concatenate([jnp.zeros((1, CX * NY * CZ), jnp.float32), source], axis=0).reshape(5, CX, NY, CZ)
        return centre - step_ratio / fraction_p[1:-1, 1:-1, 1:-1][None] * (summed - source)
    blocks = lax.map(one_slab, jnp.arange(SLABS, dtype=jnp.int32))
    new_state = jnp.transpose(blocks, (1, 0, 2, 3, 4)).reshape(5, NX, NY, CZ)
    return (new_state, new_velocity)
```

```python
import functools

import jax
import jax.numpy as jnp
from jax import lax
from jax.experimental import pallas as pl
from jax.experimental.pallas import tpu as pltpu
from jax.sharding import PartitionSpec as P

ratio_heat = 1.4
step_ratio = 0.1
struct_step = 1.0

MESH = pl.DeviceIdType.MESH
f32 = jnp.float32
bf16 = jnp.bfloat16


def conserved(rho, vel, p):
    u, v, w = vel
    energy = p * (1.0 / (ratio_heat - 1.0)) + 0.5 * rho * (u * u + v * v + w * w)
    return [rho, rho * u, rho * v, rho * w, energy]


def flux(state, vel, p, along):
    normal = vel[along]
    terms = [normal * q for q in state]
    terms[1 + along] = terms[1 + along] + p
    terms[4] = terms[4] + p * normal
    return terms


def sound(rho, p):
    return jnp.sqrt(ratio_heat * p / rho)


def face(low, high, along, keep=None):
    rho_l, vel_l, p_l, f_l, c_l = low
    rho_h, vel_h, p_h, f_h, c_h = high
    state_l, state_h = conserved(rho_l, vel_l, p_l), conserved(rho_h, vel_h, p_h)
    flux_l, flux_h = flux(state_l, vel_l, p_l, along), flux(state_h, vel_h, p_h, along)
    speed = jnp.maximum(jnp.abs(vel_l[along]) + c_l, jnp.abs(vel_h[along]) + c_h)
    aperture = 0.5 * jnp.minimum(f_l, f_h)
    if keep is not None:
        aperture = jnp.where(keep, aperture, 0.0)
    return [
        aperture * ((flux_l[k] + flux_h[k]) - speed * (state_h[k] - state_l[k]))
        for k in range(5)
    ]


def shifted(side, amount, axis):
    rho, vel, p, f, c = side
    move = lambda a: pltpu.roll(a, amount, axis)
    return (move(rho), [move(v) for v in vel], move(p), move(f), move(c))


def parts_of(value, count):
    found = []
    for _ in range(count):
        head = value.astype(bf16).astype(f32)
        found.append(head)
        value = value - head
    return found


def rows_of(rows, height):
    width = rows[0].shape[-1]
    at = lax.broadcasted_iota(jnp.int32, (height, width), 0)
    total = jnp.zeros((height, width), f32)
    for k, row in enumerate(rows):
        total = jnp.where(at == k, row, total)
    return total


def dot_nn(a, b):
    return lax.dot_general(a, b, (((1,), (0,)), ((), ())), preferred_element_type=f32)


def dot_nt(a, b):
    return lax.dot_general(a, b, (((1,), (1,)), ((), ())), preferred_element_type=f32)


def step_kernel(
    slabs,
    cols,
    rho_h,
    vel_h,
    p_h,
    code_h,
    cell_h,
    elem_h,
    count_h,
    normal_h,
    mass_h,
    removed_h,
    motion_h,
    out_h,
    new_h,
    rho_v,
    vel_v,
    p_v,
    code_v,
    cell_v,
    elem_v,
    count_v,
    normal_v,
    mass_v,
    removed_v,
    motion_v,
    halo_rho,
    halo_vel,
    halo_p,
    halo_code,
    edge_out,
    edge_in,
    loads,
    source,
    acc,
    new_full,
    new_own,
    local_sem,
    x_send,
    x_recv,
    y_send,
    y_recv,
    l_send,
    l_recv,
    out_sem,
    new_sem,
):
    bx, by, bz = rho_v.shape
    rows = cell_v.shape[-1]
    group = mass_v.shape[-1]
    share = group // cols
    s, c = lax.axis_index("slab"), lax.axis_index("col")
    has_down, has_up = s > 0, s < slabs - 1
    has_left, has_right = c > 0, c < cols - 1

    pairs = [
        (p_h, p_v),
        (code_h, code_v),
        (cell_h, cell_v),
        (rho_h, rho_v),
        (vel_h, vel_v),
        (normal_h, normal_v),
        (elem_h, elem_v),
        (count_h, count_v),
        (mass_h, mass_v),
        (removed_h, removed_v),
        (motion_h, motion_v),
    ]
    fetches = [
        pltpu.make_async_copy(src, dst, local_sem.at[i]) for i, (src, dst) in enumerate(pairs)
    ]
    for fetch in fetches:
        fetch.start()

    barrier = pltpu.get_barrier_semaphore()

    @pl.when(has_down)
    def _():
        pl.semaphore_signal(barrier, inc=1, device_id={"slab": s - 1}, device_id_type=MESH)

    @pl.when(has_up)
    def _():
        pl.semaphore_signal(barrier, inc=1, device_id={"slab": s + 1}, device_id_type=MESH)

    for step in range(1, cols):
        pl.semaphore_signal(
            barrier, inc=1, device_id={"col": lax.rem(c + step, cols)}, device_id_type=MESH
        )
    pl.semaphore_wait(
        barrier, has_down.astype(jnp.int32) + has_up.astype(jnp.int32) + (cols - 1)
    )

    def plane_copies(plane, slot, peer):
        return [
            pltpu.make_async_remote_copy(
                src_ref=src,
                dst_ref=dst.at[slot],
                send_sem=x_send.at[slot, i],
                recv_sem=x_recv.at[slot, i],
                device_id={"slab": peer},
                device_id_type=MESH,
            )
            for i, (src, dst) in enumerate(
                [
                    (vel_h.at[:, plane], halo_vel),
                    (rho_h.at[plane], halo_rho),
                    (p_h.at[plane], halo_p),
                    (code_h.at[plane], halo_code),
                ]
            )
        ]

    @pl.when(has_down)
    def _():
        for copy in plane_copies(0, 1, s - 1):
            copy.start()

    @pl.when(has_up)
    def _():
        for copy in plane_copies(bx - 1, 0, s + 1):
            copy.start()

    def blank(slot):
        halo_rho[slot] = jnp.ones((by, bz), f32)
        halo_p[slot] = jnp.ones((by, bz), f32)
        halo_vel[slot] = jnp.zeros((3, by, bz), f32)
        halo_code[slot] = jnp.zeros((by, bz), jnp.int32)

    @pl.when(jnp.logical_not(has_down))
    def _():
        blank(0)

    @pl.when(jnp.logical_not(has_up))
    def _():
        blank(1)

    for fetch in fetches:
        fetch.wait()

    for side, y in ((0, 0), (1, by - 1)):
        for x in range(bx):
            edge_out[side, 0, x : x + 1, :] = rho_v[x, y : y + 1, :]
            for k in range(3):
                edge_out[side, 1 + k, x : x + 1, :] = vel_v[k, x, y : y + 1, :]
            edge_out[side, 4, x : x + 1, :] = p_v[x, y : y + 1, :]
            edge_out[side, 5, x : x + 1, :] = code_v[x, y : y + 1, :].astype(f32) * (1.0 / 16.0)

    def edge_copy(side, slot, peer):
        return pltpu.make_async_remote_copy(
            src_ref=edge_out.at[side],
            dst_ref=edge_in.at[slot],
            send_sem=y_send.at[slot],
            recv_sem=y_recv.at[slot],
            device_id={"col": peer},
            device_id_type=MESH,
        )

    @pl.when(has_left)
    def _():
        edge_copy(0, 1, c - 1).start()

    @pl.when(has_right)
    def _():
        edge_copy(1, 0, c + 1).start()

    cells = cell_v[0]
    line = lax.shift_right_logical(cells, bz.bit_length() - 1)
    place = lax.bitwise_and(cells, bz - 1)
    at_line = lax.broadcasted_iota(jnp.int32, (bx * by, rows), 0) == line
    at_place = (lax.broadcasted_iota(jnp.int32, (bz, rows), 0) == place).astype(f32).astype(bf16)
    at_elem = (
        (lax.broadcasted_iota(jnp.int32, (group, rows), 0) == elem_v[0]).astype(f32).astype(bf16)
    )
    active = (lax.broadcasted_iota(jnp.int32, (1, rows), 1) < count_v[...]).astype(f32)

    fraction = code_v[...].astype(f32) * (1.0 / 16.0)
    wetted = (p_v[...] * (1.0 - fraction)).reshape(bx * by, bz)
    picked = dot_nn(jnp.concatenate(parts_of(wetted, 3), axis=0).astype(bf16), at_place)
    size = bx * by
    picked = picked[:size] + picked[size : 2 * size] + picked[2 * size :]
    weight = jnp.sum(jnp.where(at_line, picked, 0.0), axis=0, keepdims=True) * active
    normals = [normal_v[k, 0] for k in range(3)]
    pushes = [weight * n for n in normals]

    force = rows_of([-q for q in pushes], 8)
    force = jnp.concatenate(parts_of(force, 3) + [jnp.zeros_like(force)], axis=0).astype(bf16)
    found = dot_nt(force, at_elem)
    loads[c] = found[0:8] + found[8:16] + found[16:24]

    def load_copy(step):
        return pltpu.make_async_remote_copy(
            src_ref=loads.at[c],
            dst_ref=loads.at[c],
            send_sem=l_send.at[step - 1],
            recv_sem=l_recv.at[step - 1],
            device_id={"col": lax.rem(c + step, cols)},
            device_id_type=MESH,
        )

    for step in range(1, cols):
        load_copy(step).start()

    def spread(values):
        total = None
        for part in zip(*[parts_of(v, 2) for v in values]):
            lhs = jnp.concatenate([jnp.where(at_line, q, 0.0) for q in part], axis=0)
            found = dot_nt(lhs.astype(bf16), at_place)
            total = found if total is None else total + found
        return total.reshape(len(values), bx, by, bz)

    source[0:3] = spread(pushes)

    high = 16

    def inner(i, carry):
        at = pl.ds(pl.multiple_of(i * high, high), high)
        lane = lax.broadcasted_iota(jnp.int32, (high, bz), 1) < bz - 1
        before, upper = None, None
        for x in range(bx):
            rho, p = rho_v[x, at, :], p_v[x, at, :]
            vel = [vel_v[k, x, at, :] for k in range(3)]
            side = (rho, vel, p, code_v[x, at, :].astype(f32) * (1.0 / 16.0), sound(rho, p))
            through = face(side, shifted(side, bz - 1, 1), 2, lane)
            total = [q - pltpu.roll(q, 1, 1) for q in through]
            if before is not None:
                across = face(before, side, 0)
                for k in range(5):
                    acc[k, x - 1, at, :] = upper[k] + across[k]
                total = [total[k] - across[k] for k in range(5)]
            before, upper = side, total
        for k in range(5):
            acc[k, bx - 1, at, :] = upper[k]
        return carry

    lax.fori_loop(0, by // high, inner, 0)

    halves = bz // 128

    def inner_y(i, carry):
        x = i // halves
        at = pl.ds(pl.multiple_of((i % halves) * 128, 128), 128)
        below = lax.broadcasted_iota(jnp.int32, (by, 128), 0) < by - 1
        rho, p = rho_v[x, :, at], p_v[x, :, at]
        vel = [vel_v[k, x, :, at] for k in range(3)]
        side = (rho, vel, p, code_v[x, :, at].astype(f32) * (1.0 / 16.0), sound(rho, p))
        through = face(side, shifted(side, by - 1, 0), 1, below)
        for k in range(5):
            acc[k, x, :, at] += through[k] - pltpu.roll(through[k], 1, 0)
        return carry

    lax.fori_loop(0, bx * halves, inner_y, 0)

    def packed(ref, slot):
        rho, p = ref[slot, 0], ref[slot, 4]
        return (rho, [ref[slot, 1 + k] for k in range(3)], p, ref[slot, 5], sound(rho, p))

    @pl.when(has_left)
    def _():
        edge_copy(1, 0, c - 1).wait_recv()
        through = face(packed(edge_in, 0), packed(edge_out, 0), 1)
        for k in range(5):
            for x in range(bx):
                acc[k, x, 0:1, :] -= through[k][x : x + 1]

    @pl.when(has_right)
    def _():
        edge_copy(0, 1, c + 1).wait_recv()
        through = face(packed(edge_out, 1), packed(edge_in, 1), 1)
        for k in range(5):
            for x in range(bx):
                acc[k, x, by - 1 : by, :] += through[k][x : x + 1]

    for step in range(1, cols):
        load_copy(step).wait_recv()
    total = loads[0]
    for other in range(1, cols):
        total = total + loads[other]
    keep = 1.0 - removed_v[...].astype(f32)
    start = rows_of([motion_v[k] for k in range(3)], 8)
    moved = (start + struct_step * total / mass_v[...]) * keep
    new_full[...] = moved
    own = new_full[:, pl.ds(pl.multiple_of(c * share, share), share)]
    for k in range(3):
        new_own[k] = own[k : k + 1]
    new_copy = pltpu.make_async_copy(new_own, new_h, new_sem)
    new_copy.start()
    moved = jnp.concatenate(parts_of(moved, 3) + [jnp.zeros_like(moved)], axis=0).astype(bf16)
    found = dot_nn(moved, at_elem)
    found = found[0:8] + found[8:16] + found[16:24]
    work = jnp.sum(rows_of(normals, 8) * found, axis=0, keepdims=True)
    source[3:4] = spread([weight * work])

    def join(i, carry):
        x = i // (by // high)
        at = pl.ds(pl.multiple_of((i % (by // high)) * high, high), high)
        rho, p = rho_v[x, at, :], p_v[x, at, :]
        state = conserved(rho, [vel_v[k, x, at, :] for k in range(3)], p)
        scale = step_ratio / (code_v[x, at, :].astype(f32) * (1.0 / 16.0))
        acc[0, x, at, :] = state[0] - scale * acc[0, x, at, :]
        for k in range(4):
            acc[1 + k, x, at, :] = state[1 + k] - scale * (
                acc[1 + k, x, at, :] - source[k, x, at, :]
            )
        return carry

    lax.fori_loop(0, bx * (by // high), join, 0)

    near = lax.rem(s + 1, 2)

    def out_copy(slot):
        plane = slot * (bx - 1)
        return pltpu.make_async_copy(acc.at[:, plane], out_h.at[:, plane], out_sem.at[slot])

    for turn in range(2):
        slot = near if turn == 0 else 1 - near
        plane = slot * (bx - 1)
        sign = (1 - 2 * slot).astype(f32)

        @pl.when(jnp.logical_or(jnp.logical_and(slot == 0, has_down), jnp.logical_and(slot == 1, has_up)))
        def _():
            for copy in plane_copies(0, slot, s - 1 + 2 * slot):
                copy.wait_recv()

        def outer(i, carry):
            at = pl.ds(pl.multiple_of(i * high, high), high)
            rho, p = rho_v[plane, at, :], p_v[plane, at, :]
            vel = [vel_v[k, plane, at, :] for k in range(3)]
            own_fraction = code_v[plane, at, :].astype(f32) * (1.0 / 16.0)
            state = conserved(rho, vel, p)
            terms = flux(state, vel, p, 0)
            rho_n, p_n = halo_rho[slot, at, :], halo_p[slot, at, :]
            vel_n = [halo_vel[slot, k, at, :] for k in range(3)]
            fraction_n = halo_code[slot, at, :].astype(f32) * (1.0 / 16.0)
            state_n = conserved(rho_n, vel_n, p_n)
            terms_n = flux(state_n, vel_n, p_n, 0)
            speed = jnp.maximum(
                jnp.abs(vel[0]) + sound(rho, p), jnp.abs(vel_n[0]) + sound(rho_n, p_n)
            )
            scale = (0.5 * step_ratio) * jnp.minimum(own_fraction, fraction_n) / own_fraction
            for k in range(5):
                acc[k, plane, at, :] += scale * (
                    sign * (terms[k] + terms_n[k]) - speed * (state[k] - state_n[k])
                )
            return carry

        lax.fori_loop(0, by // high, outer, 0)
        out_copy(slot).start()

    for slot in range(2):
        out_copy(slot).wait()
    new_copy.wait()

    @pl.when(has_down)
    def _():
        for copy in plane_copies(0, 1, s - 1):
            copy.wait_send()

    @pl.when(has_up)
    def _():
        for copy in plane_copies(bx - 1, 0, s + 1):
            copy.wait_send()

    @pl.when(has_left)
    def _():
        edge_copy(0, 1, c - 1).wait_send()

    @pl.when(has_right)
    def _():
        edge_copy(1, 0, c + 1).wait_send()

    for step in range(1, cols):
        load_copy(step).wait_send()


def local(slabs, cols, *args):
    density, velocity, pressure, code, cell, elem, count, normal, mass, removed, motion = args
    bx, by, bz = density.shape
    group = mass.shape[-1]
    share = group // cols
    plane = (by, bz)
    i32 = jnp.int32
    vmem, dma = pltpu.VMEM, pltpu.SemaphoreType.DMA
    return pl.pallas_call(
        functools.partial(step_kernel, slabs, cols),
        out_shape=(
            jax.ShapeDtypeStruct((5,) + density.shape, f32),
            jax.ShapeDtypeStruct((3, 1, share), f32),
        ),
        in_specs=[pl.BlockSpec(memory_space=pl.ANY)] * len(args),
        out_specs=(pl.BlockSpec(memory_space=pl.ANY), pl.BlockSpec(memory_space=pl.ANY)),
        scratch_shapes=[vmem(a.shape, a.dtype) for a in args]
        + [
            vmem((2,) + plane, f32),
            vmem((2, 3) + plane, f32),
            vmem((2,) + plane, f32),
            vmem((2,) + plane, i32),
            vmem((2, 6, bx, bz), f32),
            vmem((2, 6, bx, bz), f32),
            vmem((cols, 8, group), f32),
            vmem((4,) + density.shape, f32),
            vmem((5,) + density.shape, f32),
            vmem((8, group), f32),
            vmem((3, 1, share), f32),
            dma((len(args),)),
            dma((2, 4)),
            dma((2, 4)),
            dma((2,)),
            dma((2,)),
            dma((max(cols - 1, 1),)),
            dma((max(cols - 1, 1),)),
            dma((2,)),
            dma,
        ],
        compiler_params=pltpu.CompilerParams(
            collective_id=0, has_side_effects=True, vmem_limit_bytes=40 * 1024 * 1024
        ),
        name="coupling_step",
    )(*args)


def solution(mesh):
    slabs, cols = mesh.shape["slab"], mesh.shape["col"]
    placed = (
        P("slab", "col", None),
        P(None, "slab", "col", None),
        P("slab", "col", None),
        P("slab", "col", None),
        P("slab", "col", None),
        P("slab", "col", None),
        P("slab", "col"),
        P(None, "slab", "col", None),
        P("slab", None),
        P("slab", None),
        P(None, "slab", None),
    )
    return jax.shard_map(
        functools.partial(local, slabs, cols),
        mesh=mesh,
        in_specs=placed,
        out_specs=(P(None, "slab", "col", None), P(None, "slab", "col")),
        check_vma=False,
    )
```

```python
import functools

import jax
import jax.numpy as jnp
from jax import lax
from jax.experimental import pallas as pl
from jax.experimental.pallas import tpu as pltpu
from jax.sharding import PartitionSpec as P

ratio_heat = 1.4
step_ratio = 0.1
struct_step = 1.0
pieces = 2

MESH = pl.DeviceIdType.MESH
f32 = jnp.float32
bf16 = jnp.bfloat16


def conserved(rho, vel, p):
    u, v, w = vel
    energy = p * (1.0 / (ratio_heat - 1.0)) + 0.5 * rho * (u * u + v * v + w * w)
    return [rho, rho * u, rho * v, rho * w, energy]


def flux(state, vel, p, along):
    normal = vel[along]
    terms = [normal * q for q in state]
    terms[1 + along] = terms[1 + along] + p
    terms[4] = terms[4] + p * normal
    return terms


def sound(rho, p):
    return jnp.sqrt(ratio_heat * p / rho)


def face(low, high, along, keep=None):
    rho_l, vel_l, p_l, f_l, c_l = low
    rho_h, vel_h, p_h, f_h, c_h = high
    state_l, state_h = conserved(rho_l, vel_l, p_l), conserved(rho_h, vel_h, p_h)
    flux_l, flux_h = flux(state_l, vel_l, p_l, along), flux(state_h, vel_h, p_h, along)
    speed = jnp.maximum(jnp.abs(vel_l[along]) + c_l, jnp.abs(vel_h[along]) + c_h)
    aperture = 0.5 * jnp.minimum(f_l, f_h)
    if keep is not None:
        aperture = jnp.where(keep, aperture, 0.0)
    return [
        aperture * ((flux_l[k] + flux_h[k]) - speed * (state_h[k] - state_l[k]))
        for k in range(5)
    ]


def shifted(side, amount, axis):
    rho, vel, p, f, c = side
    move = lambda a: pltpu.roll(a, amount, axis)
    return (move(rho), [move(v) for v in vel], move(p), move(f), move(c))


def parts_of(value, count):
    found = []
    for _ in range(count):
        head = value.astype(bf16).astype(f32)
        found.append(head)
        value = value - head
    return found


def rows_of(rows, height):
    width = rows[0].shape[-1]
    at = lax.broadcasted_iota(jnp.int32, (height, width), 0)
    total = jnp.zeros((height, width), f32)
    for k, row in enumerate(rows):
        total = jnp.where(at == k, row, total)
    return total


def dot_nn(a, b):
    return lax.dot_general(a, b, (((1,), (0,)), ((), ())), preferred_element_type=f32)


def dot_nt(a, b):
    return lax.dot_general(a, b, (((1,), (1,)), ((), ())), preferred_element_type=f32)


def step_kernel(
    slabs,
    cols,
    rho_h,
    vel_h,
    p_h,
    code_h,
    cell_h,
    elem_h,
    count_h,
    normal_h,
    mass_h,
    removed_h,
    motion_h,
    out_h,
    new_h,
    rho_v,
    vel_v,
    p_v,
    code_v,
    cell_v,
    elem_v,
    count_v,
    normal_v,
    mass_v,
    removed_v,
    motion_v,
    halo_rho,
    halo_vel,
    halo_p,
    halo_code,
    edge_out,
    edge_in,
    loads,
    source,
    acc,
    new_full,
    new_own,
    local_sem,
    x_send,
    x_recv,
    y_send,
    y_recv,
    l_send,
    l_recv,
    out_sem,
    new_sem,
):
    bx, by, bz = rho_v.shape
    rows = cell_v.shape[-1]
    group = mass_v.shape[-1]
    share = group // cols
    s, c = lax.axis_index("slab"), lax.axis_index("col")
    has_down, has_up = s > 0, s < slabs - 1
    has_left, has_right = c > 0, c < cols - 1

    pairs = [
        (p_h, p_v),
        (code_h, code_v),
        (cell_h, cell_v),
        (rho_h, rho_v),
        (vel_h, vel_v),
        (normal_h, normal_v),
        (elem_h, elem_v),
        (count_h, count_v),
        (mass_h, mass_v),
        (removed_h, removed_v),
        (motion_h, motion_v),
    ]
    fetches = [
        pltpu.make_async_copy(src, dst, local_sem.at[i]) for i, (src, dst) in enumerate(pairs)
    ]
    for fetch in fetches:
        fetch.start()

    barrier = pltpu.get_barrier_semaphore()

    @pl.when(has_down)
    def _():
        pl.semaphore_signal(barrier, inc=1, device_id={"slab": s - 1}, device_id_type=MESH)

    @pl.when(has_up)
    def _():
        pl.semaphore_signal(barrier, inc=1, device_id={"slab": s + 1}, device_id_type=MESH)

    for step in range(1, cols):
        pl.semaphore_signal(
            barrier, inc=1, device_id={"col": lax.rem(c + step, cols)}, device_id_type=MESH
        )
    pl.semaphore_wait(
        barrier, has_down.astype(jnp.int32) + has_up.astype(jnp.int32) + (cols - 1)
    )

    tall = by // pieces

    def plane_copies(way, piece, peer):
        plane, slot, at = way * (bx - 1), 1 - way, pl.ds(piece * tall, tall)
        return [
            pltpu.make_async_remote_copy(
                src_ref=src,
                dst_ref=dst,
                send_sem=x_send.at[way, piece, i],
                recv_sem=x_recv.at[slot, piece, i],
                device_id={"slab": peer},
                device_id_type=MESH,
            )
            for i, (src, dst) in enumerate(
                [
                    (vel_h.at[:, plane, at], halo_vel.at[slot, :, at]),
                    (rho_h.at[plane, at], halo_rho.at[slot, at]),
                    (p_h.at[plane, at], halo_p.at[slot, at]),
                    (code_h.at[plane, at], halo_code.at[slot, at]),
                ]
            )
        ]

    def has_way(way):
        return jnp.logical_and(s - 1 + 2 * way >= 0, s - 1 + 2 * way < slabs)

    far = lax.rem(s, 2)
    for way in (far, 1 - far):

        @pl.when(has_way(way))
        def _():
            for piece in range(pieces):
                for copy in plane_copies(way, piece, s - 1 + 2 * way):
                    copy.start()

    def blank(slot):
        halo_rho[slot] = jnp.ones((by, bz), f32)
        halo_p[slot] = jnp.ones((by, bz), f32)
        halo_vel[slot] = jnp.zeros((3, by, bz), f32)
        halo_code[slot] = jnp.zeros((by, bz), jnp.int32)

    @pl.when(jnp.logical_not(has_down))
    def _():
        blank(0)

    @pl.when(jnp.logical_not(has_up))
    def _():
        blank(1)

    for fetch in fetches:
        fetch.wait()

    for side, y in ((0, 0), (1, by - 1)):
        for x in range(bx):
            edge_out[side, 0, x : x + 1, :] = rho_v[x, y : y + 1, :]
            for k in range(3):
                edge_out[side, 1 + k, x : x + 1, :] = vel_v[k, x, y : y + 1, :]
            edge_out[side, 4, x : x + 1, :] = p_v[x, y : y + 1, :]
            edge_out[side, 5, x : x + 1, :] = code_v[x, y : y + 1, :].astype(f32) * (1.0 / 16.0)

    def edge_copy(side, slot, peer):
        return pltpu.make_async_remote_copy(
            src_ref=edge_out.at[side],
            dst_ref=edge_in.at[slot],
            send_sem=y_send.at[slot],
            recv_sem=y_recv.at[slot],
            device_id={"col": peer},
            device_id_type=MESH,
        )

    @pl.when(has_left)
    def _():
        edge_copy(0, 1, c - 1).start()

    @pl.when(has_right)
    def _():
        edge_copy(1, 0, c + 1).start()

    cells = cell_v[0]
    line = lax.shift_right_logical(cells, bz.bit_length() - 1)
    place = lax.bitwise_and(cells, bz - 1)
    at_line = lax.broadcasted_iota(jnp.int32, (bx * by, rows), 0) == line
    at_place = (lax.broadcasted_iota(jnp.int32, (bz, rows), 0) == place).astype(f32).astype(bf16)
    at_elem = (
        (lax.broadcasted_iota(jnp.int32, (group, rows), 0) == elem_v[0]).astype(f32).astype(bf16)
    )
    active = (lax.broadcasted_iota(jnp.int32, (1, rows), 1) < count_v[...]).astype(f32)

    fraction = code_v[...].astype(f32) * (1.0 / 16.0)
    wetted = (p_v[...] * (1.0 - fraction)).reshape(bx * by, bz)
    picked = dot_nn(jnp.concatenate(parts_of(wetted, 3), axis=0).astype(bf16), at_place)
    size = bx * by
    picked = picked[:size] + picked[size : 2 * size] + picked[2 * size :]
    weight = jnp.sum(jnp.where(at_line, picked, 0.0), axis=0, keepdims=True) * active
    normals = [normal_v[k, 0] for k in range(3)]
    pushes = [weight * n for n in normals]

    force = rows_of([-q for q in pushes], 8)
    force = jnp.concatenate(parts_of(force, 3) + [jnp.zeros_like(force)], axis=0).astype(bf16)
    found = dot_nt(force, at_elem)
    loads[c] = found[0:8] + found[8:16] + found[16:24]

    def load_copy(step):
        return pltpu.make_async_remote_copy(
            src_ref=loads.at[c],
            dst_ref=loads.at[c],
            send_sem=l_send.at[step - 1],
            recv_sem=l_recv.at[step - 1],
            device_id={"col": lax.rem(c + step, cols)},
            device_id_type=MESH,
        )

    for step in range(1, cols):
        load_copy(step).start()

    def spread(values):
        total = None
        for part in zip(*[parts_of(v, 2) for v in values]):
            lhs = jnp.concatenate([jnp.where(at_line, q, 0.0) for q in part], axis=0)
            found = dot_nt(lhs.astype(bf16), at_place)
            total = found if total is None else total + found
        return total.reshape(len(values), bx, by, bz)

    source[0:3] = spread(pushes)

    high = 16

    def inner(i, carry):
        at = pl.ds(pl.multiple_of(i * high, high), high)
        lane = lax.broadcasted_iota(jnp.int32, (high, bz), 1) < bz - 1
        before, upper = None, None
        for x in range(bx):
            rho, p = rho_v[x, at, :], p_v[x, at, :]
            vel = [vel_v[k, x, at, :] for k in range(3)]
            side = (rho, vel, p, code_v[x, at, :].astype(f32) * (1.0 / 16.0), sound(rho, p))
            through = face(side, shifted(side, bz - 1, 1), 2, lane)
            total = [q - pltpu.roll(q, 1, 1) for q in through]
            if before is not None:
                across = face(before, side, 0)
                for k in range(5):
                    acc[k, x - 1, at, :] = upper[k] + across[k]
                total = [total[k] - across[k] for k in range(5)]
            before, upper = side, total
        for k in range(5):
            acc[k, bx - 1, at, :] = upper[k]
        return carry

    lax.fori_loop(0, by // high, inner, 0)

    halves = bz // 128

    def inner_y(i, carry):
        x = i // halves
        at = pl.ds(pl.multiple_of((i % halves) * 128, 128), 128)
        below = lax.broadcasted_iota(jnp.int32, (by, 128), 0) < by - 1
        rho, p = rho_v[x, :, at], p_v[x, :, at]
        vel = [vel_v[k, x, :, at] for k in range(3)]
        side = (rho, vel, p, code_v[x, :, at].astype(f32) * (1.0 / 16.0), sound(rho, p))
        through = face(side, shifted(side, by - 1, 0), 1, below)
        for k in range(5):
            acc[k, x, :, at] += through[k] - pltpu.roll(through[k], 1, 0)
        return carry

    lax.fori_loop(0, bx * halves, inner_y, 0)

    def packed(ref, slot):
        rho, p = ref[slot, 0], ref[slot, 4]
        return (rho, [ref[slot, 1 + k] for k in range(3)], p, ref[slot, 5], sound(rho, p))

    @pl.when(has_left)
    def _():
        edge_copy(1, 0, c - 1).wait_recv()
        through = face(packed(edge_in, 0), packed(edge_out, 0), 1)
        for k in range(5):
            for x in range(bx):
                acc[k, x, 0:1, :] -= through[k][x : x + 1]

    @pl.when(has_right)
    def _():
        edge_copy(0, 1, c + 1).wait_recv()
        through = face(packed(edge_out, 1), packed(edge_in, 1), 1)
        for k in range(5):
            for x in range(bx):
                acc[k, x, by - 1 : by, :] += through[k][x : x + 1]

    for step in range(1, cols):
        load_copy(step).wait_recv()
    total = loads[0]
    for other in range(1, cols):
        total = total + loads[other]
    keep = 1.0 - removed_v[...].astype(f32)
    start = rows_of([motion_v[k] for k in range(3)], 8)
    moved = (start + struct_step * total / mass_v[...]) * keep
    new_full[...] = moved
    own = new_full[:, pl.ds(pl.multiple_of(c * share, share), share)]
    for k in range(3):
        new_own[k] = own[k : k + 1]
    new_copy = pltpu.make_async_copy(new_own, new_h, new_sem)
    new_copy.start()
    moved = jnp.concatenate(parts_of(moved, 3) + [jnp.zeros_like(moved)], axis=0).astype(bf16)
    found = dot_nn(moved, at_elem)
    found = found[0:8] + found[8:16] + found[16:24]
    work = jnp.sum(rows_of(normals, 8) * found, axis=0, keepdims=True)
    source[3:4] = spread([weight * work])

    def join(i, carry):
        x = i // (by // high)
        at = pl.ds(pl.multiple_of((i % (by // high)) * high, high), high)
        rho, p = rho_v[x, at, :], p_v[x, at, :]
        state = conserved(rho, [vel_v[k, x, at, :] for k in range(3)], p)
        scale = step_ratio / (code_v[x, at, :].astype(f32) * (1.0 / 16.0))
        acc[0, x, at, :] = state[0] - scale * acc[0, x, at, :]
        for k in range(4):
            acc[1 + k, x, at, :] = state[1 + k] - scale * (
                acc[1 + k, x, at, :] - source[k, x, at, :]
            )
        return carry

    lax.fori_loop(0, bx * (by // high), join, 0)

    def out_copy(slot, piece):
        plane, at = slot * (bx - 1), pl.ds(piece * tall, tall)
        return pltpu.make_async_copy(
            acc.at[:, plane, at], out_h.at[:, plane, at], out_sem.at[slot, piece]
        )

    for slot in (1 - far, far):
        plane = slot * (bx - 1)
        sign = (1 - 2 * slot).astype(f32)

        for piece in range(pieces):

            @pl.when(has_way(slot))
            def _():
                for copy in plane_copies(1 - slot, piece, s - 1 + 2 * slot):
                    copy.wait_recv()

            def outer(i, carry):
                at = pl.ds(pl.multiple_of(piece * tall + i * high, high), high)
                rho, p = rho_v[plane, at, :], p_v[plane, at, :]
                vel = [vel_v[k, plane, at, :] for k in range(3)]
                own_fraction = code_v[plane, at, :].astype(f32) * (1.0 / 16.0)
                state = conserved(rho, vel, p)
                terms = flux(state, vel, p, 0)
                rho_n, p_n = halo_rho[slot, at, :], halo_p[slot, at, :]
                vel_n = [halo_vel[slot, k, at, :] for k in range(3)]
                fraction_n = halo_code[slot, at, :].astype(f32) * (1.0 / 16.0)
                state_n = conserved(rho_n, vel_n, p_n)
                terms_n = flux(state_n, vel_n, p_n, 0)
                speed = jnp.maximum(
                    jnp.abs(vel[0]) + sound(rho, p), jnp.abs(vel_n[0]) + sound(rho_n, p_n)
                )
                scale = (0.5 * step_ratio) * jnp.minimum(own_fraction, fraction_n) / own_fraction
                for k in range(5):
                    acc[k, plane, at, :] += scale * (
                        sign * (terms[k] + terms_n[k]) - speed * (state[k] - state_n[k])
                    )
                return carry

            lax.fori_loop(0, tall // high, outer, 0)
            out_copy(slot, piece).start()

    for slot in range(2):
        for piece in range(pieces):
            out_copy(slot, piece).wait()
    new_copy.wait()

    for way in range(2):

        @pl.when(has_way(way))
        def _():
            for piece in range(pieces):
                for copy in plane_copies(way, piece, s - 1 + 2 * way):
                    copy.wait_send()

    @pl.when(has_left)
    def _():
        edge_copy(0, 1, c - 1).wait_send()

    @pl.when(has_right)
    def _():
        edge_copy(1, 0, c + 1).wait_send()

    for step in range(1, cols):
        load_copy(step).wait_send()


def place_kernel(state, new, state_out, new_out, sem):
    copies = [
        pltpu.make_async_copy(state, state_out, sem.at[0]),
        pltpu.make_async_copy(new, new_out, sem.at[1]),
    ]
    for copy in copies:
        copy.start()
    for copy in copies:
        copy.wait()


def place(state, new):
    return pl.pallas_call(
        place_kernel,
        out_shape=tuple(jax.ShapeDtypeStruct(a.shape, a.dtype) for a in (state, new)),
        in_specs=[pl.BlockSpec(memory_space=pl.ANY)] * 2,
        out_specs=(pl.BlockSpec(memory_space=pl.ANY),) * 2,
        scratch_shapes=[pltpu.SemaphoreType.DMA((2,))],
        name="place_results",
    )(state, new)


def local(slabs, cols, *args):
    density, velocity, pressure, code, cell, elem, count, normal, mass, removed, motion = args
    bx, by, bz = density.shape
    group = mass.shape[-1]
    share = group // cols
    plane = (by, bz)
    i32 = jnp.int32
    vmem, dma = pltpu.VMEM, pltpu.SemaphoreType.DMA
    args = [pltpu.with_memory_space_constraint(a, pltpu.HBM) if a.size > 1 else a for a in args]
    return place(*pl.pallas_call(
        functools.partial(step_kernel, slabs, cols),
        out_shape=(
            jax.ShapeDtypeStruct((5,) + density.shape, f32),
            jax.ShapeDtypeStruct((3, 1, share), f32),
        ),
        in_specs=[pl.BlockSpec(memory_space=pltpu.HBM)] * len(args),
        out_specs=(pl.BlockSpec(memory_space=pl.ANY), pl.BlockSpec(memory_space=pl.ANY)),
        scratch_shapes=[vmem(a.shape, a.dtype) for a in args]
        + [
            vmem((2,) + plane, f32),
            vmem((2, 3) + plane, f32),
            vmem((2,) + plane, f32),
            vmem((2,) + plane, i32),
            vmem((2, 6, bx, bz), f32),
            vmem((2, 6, bx, bz), f32),
            vmem((cols, 8, group), f32),
            vmem((4,) + density.shape, f32),
            vmem((5,) + density.shape, f32),
            vmem((8, group), f32),
            vmem((3, 1, share), f32),
            dma((len(args),)),
            dma((2, pieces, 4)),
            dma((2, pieces, 4)),
            dma((2,)),
            dma((2,)),
            dma((max(cols - 1, 1),)),
            dma((max(cols - 1, 1),)),
            dma((2, pieces)),
            dma,
        ],
        compiler_params=pltpu.CompilerParams(
            collective_id=0, has_side_effects=True, vmem_limit_bytes=16 * 1024 * 1024
        ),
        name="coupling_step",
    )(*args))


def solution(mesh):
    slabs, cols = mesh.shape["slab"], mesh.shape["col"]
    placed = (
        P("slab", "col", None),
        P(None, "slab", "col", None),
        P("slab", "col", None),
        P("slab", "col", None),
        P("slab", "col", None),
        P("slab", "col", None),
        P("slab", "col"),
        P(None, "slab", "col", None),
        P("slab", None),
        P("slab", None),
        P(None, "slab", None),
    )
    return jax.shard_map(
        functools.partial(local, slabs, cols),
        mesh=mesh,
        in_specs=placed,
        out_specs=(P(None, "slab", "col", None), P(None, "slab", "col")),
        check_vma=False,
    )
```

```python
import functools

import jax
import jax.numpy as jnp
from jax import lax
from jax.experimental import pallas as pl
from jax.experimental.pallas import tpu as pltpu
from jax.sharding import PartitionSpec as P

ratio_heat = 1.4
step_ratio = 0.1
struct_step = 1.0
pieces = 2

MESH = pl.DeviceIdType.MESH
f32 = jnp.float32
bf16 = jnp.bfloat16


def conserved(rho, vel, p):
    u, v, w = vel
    energy = p * (1.0 / (ratio_heat - 1.0)) + 0.5 * rho * (u * u + v * v + w * w)
    return [rho, rho * u, rho * v, rho * w, energy]


def flux(state, vel, p, along):
    normal = vel[along]
    terms = [normal * q for q in state]
    terms[1 + along] = terms[1 + along] + p
    terms[4] = terms[4] + p * normal
    return terms


def sound(rho, p):
    return jnp.sqrt(ratio_heat * p / rho)


def face(low, high, along, keep=None):
    rho_l, vel_l, p_l, f_l, c_l = low
    rho_h, vel_h, p_h, f_h, c_h = high
    state_l, state_h = conserved(rho_l, vel_l, p_l), conserved(rho_h, vel_h, p_h)
    flux_l, flux_h = flux(state_l, vel_l, p_l, along), flux(state_h, vel_h, p_h, along)
    speed = jnp.maximum(jnp.abs(vel_l[along]) + c_l, jnp.abs(vel_h[along]) + c_h)
    aperture = 0.5 * jnp.minimum(f_l, f_h)
    if keep is not None:
        aperture = jnp.where(keep, aperture, 0.0)
    return [
        aperture * ((flux_l[k] + flux_h[k]) - speed * (state_h[k] - state_l[k]))
        for k in range(5)
    ]


def shifted(side, amount, axis):
    rho, vel, p, f, c = side
    move = lambda a: pltpu.roll(a, amount, axis)
    return (move(rho), [move(v) for v in vel], move(p), move(f), move(c))


def parts_of(value, count):
    found = []
    for _ in range(count):
        head = value.astype(bf16).astype(f32)
        found.append(head)
        value = value - head
    return found


def rows_of(rows, height):
    width = rows[0].shape[-1]
    at = lax.broadcasted_iota(jnp.int32, (height, width), 0)
    total = jnp.zeros((height, width), f32)
    for k, row in enumerate(rows):
        total = jnp.where(at == k, row, total)
    return total


def dot_nn(a, b):
    return lax.dot_general(a, b, (((1,), (0,)), ((), ())), preferred_element_type=f32)


def dot_nt(a, b):
    return lax.dot_general(a, b, (((1,), (1,)), ((), ())), preferred_element_type=f32)


def step_kernel(
    slabs,
    cols,
    rho_h,
    vel_h,
    p_h,
    code_h,
    cell_h,
    elem_h,
    count_h,
    normal_h,
    mass_h,
    removed_h,
    motion_h,
    out_h,
    new_h,
    rho_v,
    vel_v,
    p_v,
    code_v,
    cell_v,
    elem_v,
    count_v,
    normal_v,
    mass_v,
    removed_v,
    motion_v,
    halo_rho,
    halo_vel,
    halo_p,
    halo_code,
    edge_out,
    edge_in,
    loads,
    source,
    acc,
    new_full,
    new_own,
    local_sem,
    x_send,
    x_recv,
    y_send,
    y_recv,
    l_send,
    l_recv,
    out_sem,
    new_sem,
):
    bx, by, bz = rho_v.shape
    rows = cell_v.shape[-1]
    group = mass_v.shape[-1]
    share = group // cols
    s, c = lax.axis_index("slab"), lax.axis_index("col")
    has_down, has_up = s > 0, s < slabs - 1
    has_left, has_right = c > 0, c < cols - 1

    pairs = [
        (p_h, p_v),
        (code_h, code_v),
        (cell_h, cell_v),
        (rho_h, rho_v),
        (vel_h, vel_v),
        (normal_h, normal_v),
        (elem_h, elem_v),
        (count_h, count_v),
        (mass_h, mass_v),
        (removed_h, removed_v),
        (motion_h, motion_v),
    ]
    fetches = [
        pltpu.make_async_copy(src, dst, local_sem.at[i]) for i, (src, dst) in enumerate(pairs)
    ]
    for fetch in fetches:
        fetch.start()

    barrier = pltpu.get_barrier_semaphore()

    @pl.when(has_down)
    def _():
        pl.semaphore_signal(barrier, inc=1, device_id={"slab": s - 1}, device_id_type=MESH)

    @pl.when(has_up)
    def _():
        pl.semaphore_signal(barrier, inc=1, device_id={"slab": s + 1}, device_id_type=MESH)

    for step in range(1, cols):
        pl.semaphore_signal(
            barrier, inc=1, device_id={"col": lax.rem(c + step, cols)}, device_id_type=MESH
        )
    pl.semaphore_wait(
        barrier, has_down.astype(jnp.int32) + has_up.astype(jnp.int32) + (cols - 1)
    )

    tall = by // pieces

    def plane_copies(way, piece, peer):
        plane, slot, at = way * (bx - 1), 1 - way, pl.ds(piece * tall, tall)
        return [
            pltpu.make_async_remote_copy(
                src_ref=src,
                dst_ref=dst,
                send_sem=x_send.at[way, piece, i],
                recv_sem=x_recv.at[slot, piece, i],
                device_id={"slab": peer},
                device_id_type=MESH,
            )
            for i, (src, dst) in enumerate(
                [
                    (vel_h.at[:, plane, at], halo_vel.at[slot, :, at]),
                    (rho_h.at[plane, at], halo_rho.at[slot, at]),
                    (p_h.at[plane, at], halo_p.at[slot, at]),
                    (code_h.at[plane, at], halo_code.at[slot, at]),
                ]
            )
        ]

    def has_way(way):
        return jnp.logical_and(s - 1 + 2 * way >= 0, s - 1 + 2 * way < slabs)

    far = lax.rem(s, 2)
    for way in (far, 1 - far):

        @pl.when(has_way(way))
        def _():
            for piece in range(pieces):
                for copy in plane_copies(way, piece, s - 1 + 2 * way):
                    copy.start()

    def blank(slot):
        halo_rho[slot] = jnp.ones((by, bz), f32)
        halo_p[slot] = jnp.ones((by, bz), f32)
        halo_vel[slot] = jnp.zeros((3, by, bz), f32)
        halo_code[slot] = jnp.zeros((by, bz), jnp.int32)

    @pl.when(jnp.logical_not(has_down))
    def _():
        blank(0)

    @pl.when(jnp.logical_not(has_up))
    def _():
        blank(1)

    for fetch in fetches:
        fetch.wait()

    for side, y in ((0, 0), (1, by - 1)):
        for x in range(bx):
            edge_out[side, 0, x : x + 1, :] = rho_v[x, y : y + 1, :]
            for k in range(3):
                edge_out[side, 1 + k, x : x + 1, :] = vel_v[k, x, y : y + 1, :]
            edge_out[side, 4, x : x + 1, :] = p_v[x, y : y + 1, :]
            edge_out[side, 5, x : x + 1, :] = code_v[x, y : y + 1, :].astype(f32) * (1.0 / 16.0)

    def edge_copy(side, slot, peer):
        return pltpu.make_async_remote_copy(
            src_ref=edge_out.at[side],
            dst_ref=edge_in.at[slot],
            send_sem=y_send.at[slot],
            recv_sem=y_recv.at[slot],
            device_id={"col": peer},
            device_id_type=MESH,
        )

    @pl.when(has_left)
    def _():
        edge_copy(0, 1, c - 1).start()

    @pl.when(has_right)
    def _():
        edge_copy(1, 0, c + 1).start()

    cells = cell_v[0]
    line = lax.shift_right_logical(cells, bz.bit_length() - 1)
    place = lax.bitwise_and(cells, bz - 1)
    at_line = lax.broadcasted_iota(jnp.int32, (bx * by, rows), 0) == line
    at_place = (lax.broadcasted_iota(jnp.int32, (bz, rows), 0) == place).astype(f32).astype(bf16)
    at_elem = (
        (lax.broadcasted_iota(jnp.int32, (group, rows), 0) == elem_v[0]).astype(f32).astype(bf16)
    )
    active = (lax.broadcasted_iota(jnp.int32, (1, rows), 1) < count_v[...]).astype(f32)

    fraction = code_v[...].astype(f32) * (1.0 / 16.0)
    wetted = (p_v[...] * (1.0 - fraction)).reshape(bx * by, bz)
    picked = dot_nn(jnp.concatenate(parts_of(wetted, 3), axis=0).astype(bf16), at_place)
    size = bx * by
    picked = picked[:size] + picked[size : 2 * size] + picked[2 * size :]
    weight = jnp.sum(jnp.where(at_line, picked, 0.0), axis=0, keepdims=True) * active
    normals = [normal_v[k, 0] for k in range(3)]
    pushes = [weight * n for n in normals]

    force = rows_of([-q for q in pushes], 8)
    force = jnp.concatenate(parts_of(force, 3) + [jnp.zeros_like(force)], axis=0).astype(bf16)
    found = dot_nt(force, at_elem)
    loads[c] = found[0:8] + found[8:16] + found[16:24]

    def load_copy(step):
        return pltpu.make_async_remote_copy(
            src_ref=loads.at[c],
            dst_ref=loads.at[c],
            send_sem=l_send.at[step - 1],
            recv_sem=l_recv.at[step - 1],
            device_id={"col": lax.rem(c + step, cols)},
            device_id_type=MESH,
        )

    for step in range(1, cols):
        load_copy(step).start()

    def spread(values):
        total = None
        for part in zip(*[parts_of(v, 2) for v in values]):
            lhs = jnp.concatenate([jnp.where(at_line, q, 0.0) for q in part], axis=0)
            found = dot_nt(lhs.astype(bf16), at_place)
            total = found if total is None else total + found
        return total.reshape(len(values), bx, by, bz)

    source[0:3] = spread(pushes)

    high = 16

    def inner(i, carry):
        at = pl.ds(pl.multiple_of(i * high, high), high)
        lane = lax.broadcasted_iota(jnp.int32, (high, bz), 1) < bz - 1
        before, upper = None, None
        for x in range(bx):
            rho, p = rho_v[x, at, :], p_v[x, at, :]
            vel = [vel_v[k, x, at, :] for k in range(3)]
            side = (rho, vel, p, code_v[x, at, :].astype(f32) * (1.0 / 16.0), sound(rho, p))
            through = face(side, shifted(side, bz - 1, 1), 2, lane)
            total = [q - pltpu.roll(q, 1, 1) for q in through]
            if before is not None:
                across = face(before, side, 0)
                for k in range(5):
                    acc[k, x - 1, at, :] = upper[k] + across[k]
                total = [total[k] - across[k] for k in range(5)]
            before, upper = side, total
        for k in range(5):
            acc[k, bx - 1, at, :] = upper[k]
        return carry

    lax.fori_loop(0, by // high, inner, 0)

    halves = bz // 128

    def inner_y(i, carry):
        x = i // halves
        at = pl.ds(pl.multiple_of((i % halves) * 128, 128), 128)
        below = lax.broadcasted_iota(jnp.int32, (by, 128), 0) < by - 1
        rho, p = rho_v[x, :, at], p_v[x, :, at]
        vel = [vel_v[k, x, :, at] for k in range(3)]
        side = (rho, vel, p, code_v[x, :, at].astype(f32) * (1.0 / 16.0), sound(rho, p))
        through = face(side, shifted(side, by - 1, 0), 1, below)
        for k in range(5):
            acc[k, x, :, at] += through[k] - pltpu.roll(through[k], 1, 0)
        return carry

    lax.fori_loop(0, bx * halves, inner_y, 0)

    def packed(ref, slot):
        rho, p = ref[slot, 0], ref[slot, 4]
        return (rho, [ref[slot, 1 + k] for k in range(3)], p, ref[slot, 5], sound(rho, p))

    @pl.when(has_left)
    def _():
        edge_copy(1, 0, c - 1).wait_recv()
        through = face(packed(edge_in, 0), packed(edge_out, 0), 1)
        for k in range(5):
            for x in range(bx):
                acc[k, x, 0:1, :] -= through[k][x : x + 1]

    @pl.when(has_right)
    def _():
        edge_copy(0, 1, c + 1).wait_recv()
        through = face(packed(edge_out, 1), packed(edge_in, 1), 1)
        for k in range(5):
            for x in range(bx):
                acc[k, x, by - 1 : by, :] += through[k][x : x + 1]

    for step in range(1, cols):
        load_copy(step).wait_recv()
    total = loads[0]
    for other in range(1, cols):
        total = total + loads[other]
    keep = 1.0 - removed_v[...].astype(f32)
    start = rows_of([motion_v[k] for k in range(3)], 8)
    moved = (start + struct_step * total / mass_v[...]) * keep
    new_full[...] = moved
    own = new_full[:, pl.ds(pl.multiple_of(c * share, share), share)]
    for k in range(3):
        new_own[k] = own[k : k + 1]
    new_copy = pltpu.make_async_copy(new_own, new_h, new_sem)
    new_copy.start()
    moved = jnp.concatenate(parts_of(moved, 3) + [jnp.zeros_like(moved)], axis=0).astype(bf16)
    found = dot_nn(moved, at_elem)
    found = found[0:8] + found[8:16] + found[16:24]
    work = jnp.sum(rows_of(normals, 8) * found, axis=0, keepdims=True)
    source[3:4] = spread([weight * work])

    def join(i, carry):
        x = i // (by // high)
        at = pl.ds(pl.multiple_of((i % (by // high)) * high, high), high)
        rho, p = rho_v[x, at, :], p_v[x, at, :]
        state = conserved(rho, [vel_v[k, x, at, :] for k in range(3)], p)
        scale = step_ratio / (code_v[x, at, :].astype(f32) * (1.0 / 16.0))
        acc[0, x, at, :] = state[0] - scale * acc[0, x, at, :]
        for k in range(4):
            acc[1 + k, x, at, :] = state[1 + k] - scale * (
                acc[1 + k, x, at, :] - source[k, x, at, :]
            )
        return carry

    lax.fori_loop(0, bx * (by // high), join, 0)

    def out_copy(slot, piece):
        plane, at = slot * (bx - 1), pl.ds(piece * tall, tall)
        return pltpu.make_async_copy(
            acc.at[:, plane, at], out_h.at[:, plane, at], out_sem.at[slot, piece]
        )

    for slot in (1 - far, far):
        plane = slot * (bx - 1)
        sign = (1 - 2 * slot).astype(f32)

        for piece in range(pieces):

            @pl.when(has_way(slot))
            def _():
                for copy in plane_copies(1 - slot, piece, s - 1 + 2 * slot):
                    copy.wait_recv()

            def outer(i, carry):
                at = pl.ds(pl.multiple_of(piece * tall + i * high, high), high)
                rho, p = rho_v[plane, at, :], p_v[plane, at, :]
                vel = [vel_v[k, plane, at, :] for k in range(3)]
                own_fraction = code_v[plane, at, :].astype(f32) * (1.0 / 16.0)
                state = conserved(rho, vel, p)
                terms = flux(state, vel, p, 0)
                rho_n, p_n = halo_rho[slot, at, :], halo_p[slot, at, :]
                vel_n = [halo_vel[slot, k, at, :] for k in range(3)]
                fraction_n = halo_code[slot, at, :].astype(f32) * (1.0 / 16.0)
                state_n = conserved(rho_n, vel_n, p_n)
                terms_n = flux(state_n, vel_n, p_n, 0)
                speed = jnp.maximum(
                    jnp.abs(vel[0]) + sound(rho, p), jnp.abs(vel_n[0]) + sound(rho_n, p_n)
                )
                scale = (0.5 * step_ratio) * jnp.minimum(own_fraction, fraction_n) / own_fraction
                for k in range(5):
                    acc[k, plane, at, :] += scale * (
                        sign * (terms[k] + terms_n[k]) - speed * (state[k] - state_n[k])
                    )
                return carry

            lax.fori_loop(0, tall // high, outer, 0)
            out_copy(slot, piece).start()

    for slot in range(2):
        for piece in range(pieces):
            out_copy(slot, piece).wait()
    new_copy.wait()

    for way in range(2):

        @pl.when(has_way(way))
        def _():
            for piece in range(pieces):
                for copy in plane_copies(way, piece, s - 1 + 2 * way):
                    copy.wait_send()

    @pl.when(has_left)
    def _():
        edge_copy(0, 1, c - 1).wait_send()

    @pl.when(has_right)
    def _():
        edge_copy(1, 0, c + 1).wait_send()

    for step in range(1, cols):
        load_copy(step).wait_send()


def place_kernel(state, new, state_out, new_out, sem):
    copies = [
        pltpu.make_async_copy(state, state_out, sem.at[0]),
        pltpu.make_async_copy(new, new_out, sem.at[1]),
    ]
    for copy in copies:
        copy.start()
    for copy in copies:
        copy.wait()


def place(state, new):
    return pl.pallas_call(
        place_kernel,
        out_shape=tuple(jax.ShapeDtypeStruct(a.shape, a.dtype) for a in (state, new)),
        in_specs=[pl.BlockSpec(memory_space=pl.ANY)] * 2,
        out_specs=(pl.BlockSpec(memory_space=pl.ANY),) * 2,
        scratch_shapes=[pltpu.SemaphoreType.DMA((2,))],
        compiler_params=pltpu.CompilerParams(vmem_limit_bytes=4 * 1024 * 1024),
        name="place_results",
    )(state, new)


def local(slabs, cols, *args):
    density, velocity, pressure, code, cell, elem, count, normal, mass, removed, motion = args
    bx, by, bz = density.shape
    group = mass.shape[-1]
    share = group // cols
    plane = (by, bz)
    i32 = jnp.int32
    vmem, dma = pltpu.VMEM, pltpu.SemaphoreType.DMA
    args = [pltpu.with_memory_space_constraint(a, pltpu.HBM) if a.size > 1 else a for a in args]
    return place(*pl.pallas_call(
        functools.partial(step_kernel, slabs, cols),
        out_shape=(
            jax.ShapeDtypeStruct((5,) + density.shape, f32),
            jax.ShapeDtypeStruct((3, 1, share), f32),
        ),
        in_specs=[pl.BlockSpec(memory_space=pltpu.HBM)] * len(args),
        out_specs=(pl.BlockSpec(memory_space=pl.ANY), pl.BlockSpec(memory_space=pl.ANY)),
        scratch_shapes=[vmem(a.shape, a.dtype) for a in args]
        + [
            vmem((2,) + plane, f32),
            vmem((2, 3) + plane, f32),
            vmem((2,) + plane, f32),
            vmem((2,) + plane, i32),
            vmem((2, 6, bx, bz), f32),
            vmem((2, 6, bx, bz), f32),
            vmem((cols, 8, group), f32),
            vmem((4,) + density.shape, f32),
            vmem((5,) + density.shape, f32),
            vmem((8, group), f32),
            vmem((3, 1, share), f32),
            dma((len(args),)),
            dma((2, pieces, 4)),
            dma((2, pieces, 4)),
            dma((2,)),
            dma((2,)),
            dma((max(cols - 1, 1),)),
            dma((max(cols - 1, 1),)),
            dma((2, pieces)),
            dma,
        ],
        compiler_params=pltpu.CompilerParams(
            collective_id=0, has_side_effects=True, vmem_limit_bytes=16 * 1024 * 1024
        ),
        name="coupling_step",
    )(*args))


def solution(mesh):
    slabs, cols = mesh.shape["slab"], mesh.shape["col"]
    placed = (
        P("slab", "col", None),
        P(None, "slab", "col", None),
        P("slab", "col", None),
        P("slab", "col", None),
        P("slab", "col", None),
        P("slab", "col", None),
        P("slab", "col"),
        P(None, "slab", "col", None),
        P("slab", None),
        P("slab", None),
        P(None, "slab", None),
    )
    return jax.shard_map(
        functools.partial(local, slabs, cols),
        mesh=mesh,
        in_specs=placed,
        out_specs=(P(None, "slab", "col", None), P(None, "slab", "col")),
        check_vma=False,
    )
```

```python
import functools

import jax
import jax.numpy as jnp
from jax import lax
from jax.experimental import pallas as pl
from jax.experimental.pallas import tpu as pltpu
from jax.sharding import PartitionSpec as P

ratio_heat = 1.4
step_ratio = 0.1
struct_step = 1.0
pieces = 2

MESH = pl.DeviceIdType.MESH
f32 = jnp.float32
bf16 = jnp.bfloat16


def conserved(rho, vel, p):
    u, v, w = vel
    energy = p * (1.0 / (ratio_heat - 1.0)) + 0.5 * rho * (u * u + v * v + w * w)
    return [rho, rho * u, rho * v, rho * w, energy]


def flux(state, vel, p, along):
    normal = vel[along]
    terms = [normal * q for q in state]
    terms[1 + along] = terms[1 + along] + p
    terms[4] = terms[4] + p * normal
    return terms


def sound(rho, p):
    return jnp.sqrt(ratio_heat * p / rho)


def face(low, high, along, keep=None):
    rho_l, vel_l, p_l, f_l, c_l = low
    rho_h, vel_h, p_h, f_h, c_h = high
    state_l, state_h = conserved(rho_l, vel_l, p_l), conserved(rho_h, vel_h, p_h)
    flux_l, flux_h = flux(state_l, vel_l, p_l, along), flux(state_h, vel_h, p_h, along)
    speed = jnp.maximum(jnp.abs(vel_l[along]) + c_l, jnp.abs(vel_h[along]) + c_h)
    aperture = 0.5 * jnp.minimum(f_l, f_h)
    if keep is not None:
        aperture = jnp.where(keep, aperture, 0.0)
    return [
        aperture * ((flux_l[k] + flux_h[k]) - speed * (state_h[k] - state_l[k]))
        for k in range(5)
    ]


def shifted(side, amount, axis):
    rho, vel, p, f, c = side
    move = lambda a: pltpu.roll(a, amount, axis)
    return (move(rho), [move(v) for v in vel], move(p), move(f), move(c))


def parts_of(value, count):
    found = []
    for _ in range(count):
        head = value.astype(bf16).astype(f32)
        found.append(head)
        value = value - head
    return found


def rows_of(rows, height):
    width = rows[0].shape[-1]
    at = lax.broadcasted_iota(jnp.int32, (height, width), 0)
    total = jnp.zeros((height, width), f32)
    for k, row in enumerate(rows):
        total = jnp.where(at == k, row, total)
    return total


def dot_nn(a, b):
    return lax.dot_general(a, b, (((1,), (0,)), ((), ())), preferred_element_type=f32)


def dot_nt(a, b):
    return lax.dot_general(a, b, (((1,), (1,)), ((), ())), preferred_element_type=f32)


def step_kernel(
    slabs,
    cols,
    rho_h,
    vel_h,
    p_h,
    code_h,
    cell_h,
    elem_h,
    count_h,
    normal_h,
    mass_h,
    removed_h,
    motion_h,
    out_h,
    new_h,
    rho_v,
    vel_v,
    p_v,
    code_v,
    cell_v,
    elem_v,
    count_v,
    normal_v,
    mass_v,
    removed_v,
    motion_v,
    halo_rho,
    halo_vel,
    halo_p,
    halo_code,
    edge_out,
    edge_in,
    loads,
    source,
    acc,
    new_full,
    new_own,
    local_sem,
    x_send,
    x_recv,
    y_send,
    y_recv,
    l_send,
    l_recv,
    out_sem,
    new_sem,
):
    bx, by, bz = rho_v.shape
    rows = cell_v.shape[-1]
    group = mass_v.shape[-1]
    share = group // cols
    s, c = lax.axis_index("slab"), lax.axis_index("col")
    has_down, has_up = s > 0, s < slabs - 1
    has_left, has_right = c > 0, c < cols - 1

    pairs = [
        (p_h, p_v),
        (code_h, code_v),
        (cell_h, cell_v),
        (rho_h, rho_v),
        (vel_h, vel_v),
        (normal_h, normal_v),
        (elem_h, elem_v),
        (count_h, count_v),
        (mass_h, mass_v),
        (removed_h, removed_v),
        (motion_h, motion_v),
    ]
    fetches = [
        pltpu.make_async_copy(src, dst, local_sem.at[i]) for i, (src, dst) in enumerate(pairs)
    ]
    barrier = pltpu.get_barrier_semaphore()

    @pl.when(has_down)
    def _():
        pl.semaphore_signal(barrier, inc=1, device_id={"slab": s - 1}, device_id_type=MESH)

    @pl.when(has_up)
    def _():
        pl.semaphore_signal(barrier, inc=1, device_id={"slab": s + 1}, device_id_type=MESH)

    for step in range(1, cols):
        pl.semaphore_signal(
            barrier, inc=1, device_id={"col": lax.rem(c + step, cols)}, device_id_type=MESH
        )
    for fetch in fetches:
        fetch.start()
    pl.semaphore_wait(
        barrier, has_down.astype(jnp.int32) + has_up.astype(jnp.int32) + (cols - 1)
    )

    tall = by // pieces

    def plane_copies(way, piece, peer):
        plane, slot, at = way * (bx - 1), 1 - way, pl.ds(piece * tall, tall)
        return [
            pltpu.make_async_remote_copy(
                src_ref=src,
                dst_ref=dst,
                send_sem=x_send.at[way, piece, i],
                recv_sem=x_recv.at[slot, piece, i],
                device_id={"slab": peer},
                device_id_type=MESH,
            )
            for i, (src, dst) in enumerate(
                [
                    (vel_h.at[:, plane, at], halo_vel.at[slot, :, at]),
                    (rho_h.at[plane, at], halo_rho.at[slot, at]),
                    (p_h.at[plane, at], halo_p.at[slot, at]),
                    (code_h.at[plane, at], halo_code.at[slot, at]),
                ]
            )
        ]

    def has_way(way):
        return jnp.logical_and(s - 1 + 2 * way >= 0, s - 1 + 2 * way < slabs)

    def send_planes(way):
        @pl.when(has_way(way))
        def _():
            for piece in range(pieces):
                for copy in plane_copies(way, piece, s - 1 + 2 * way):
                    copy.start()

    far = lax.rem(s, 2)
    send_planes(far)

    def blank(slot):
        halo_rho[slot] = jnp.ones((by, bz), f32)
        halo_p[slot] = jnp.ones((by, bz), f32)
        halo_vel[slot] = jnp.zeros((3, by, bz), f32)
        halo_code[slot] = jnp.zeros((by, bz), jnp.int32)

    @pl.when(jnp.logical_not(has_down))
    def _():
        blank(0)

    @pl.when(jnp.logical_not(has_up))
    def _():
        blank(1)

    for fetch in fetches:
        fetch.wait()

    for side, y in ((0, 0), (1, by - 1)):
        for x in range(bx):
            edge_out[side, 0, x : x + 1, :] = rho_v[x, y : y + 1, :]
            for k in range(3):
                edge_out[side, 1 + k, x : x + 1, :] = vel_v[k, x, y : y + 1, :]
            edge_out[side, 4, x : x + 1, :] = p_v[x, y : y + 1, :]
            edge_out[side, 5, x : x + 1, :] = code_v[x, y : y + 1, :].astype(f32) * (1.0 / 16.0)

    def edge_copy(side, slot, peer):
        return pltpu.make_async_remote_copy(
            src_ref=edge_out.at[side],
            dst_ref=edge_in.at[slot],
            send_sem=y_send.at[slot],
            recv_sem=y_recv.at[slot],
            device_id={"col": peer},
            device_id_type=MESH,
        )

    @pl.when(has_left)
    def _():
        edge_copy(0, 1, c - 1).start()

    @pl.when(has_right)
    def _():
        edge_copy(1, 0, c + 1).start()

    cells = cell_v[0]
    line = lax.shift_right_logical(cells, bz.bit_length() - 1)
    place = lax.bitwise_and(cells, bz - 1)
    at_line = lax.broadcasted_iota(jnp.int32, (bx * by, rows), 0) == line
    at_place = (lax.broadcasted_iota(jnp.int32, (bz, rows), 0) == place).astype(f32).astype(bf16)
    at_elem = (
        (lax.broadcasted_iota(jnp.int32, (group, rows), 0) == elem_v[0]).astype(f32).astype(bf16)
    )
    active = (lax.broadcasted_iota(jnp.int32, (1, rows), 1) < count_v[...]).astype(f32)

    fraction = code_v[...].astype(f32) * (1.0 / 16.0)
    wetted = (p_v[...] * (1.0 - fraction)).reshape(bx * by, bz)
    picked = dot_nn(jnp.concatenate(parts_of(wetted, 3), axis=0).astype(bf16), at_place)
    size = bx * by
    picked = picked[:size] + picked[size : 2 * size] + picked[2 * size :]
    weight = jnp.sum(jnp.where(at_line, picked, 0.0), axis=0, keepdims=True) * active
    normals = [normal_v[k, 0] for k in range(3)]
    pushes = [weight * n for n in normals]

    force = rows_of([-q for q in pushes], 8)
    force = jnp.concatenate(parts_of(force, 3) + [jnp.zeros_like(force)], axis=0).astype(bf16)
    found = dot_nt(force, at_elem)
    loads[c] = found[0:8] + found[8:16] + found[16:24]

    def load_copy(step):
        return pltpu.make_async_remote_copy(
            src_ref=loads.at[c],
            dst_ref=loads.at[c],
            send_sem=l_send.at[step - 1],
            recv_sem=l_recv.at[step - 1],
            device_id={"col": lax.rem(c + step, cols)},
            device_id_type=MESH,
        )

    for step in range(1, cols):
        load_copy(step).start()
    send_planes(1 - far)

    def spread(values):
        total = None
        for part in zip(*[parts_of(v, 2) for v in values]):
            lhs = jnp.concatenate([jnp.where(at_line, q, 0.0) for q in part], axis=0)
            found = dot_nt(lhs.astype(bf16), at_place)
            total = found if total is None else total + found
        return total.reshape(len(values), bx, by, bz)

    source[0:3] = spread(pushes)

    high = 16

    def inner(i, carry):
        at = pl.ds(pl.multiple_of(i * high, high), high)
        lane = lax.broadcasted_iota(jnp.int32, (high, bz), 1) < bz - 1
        before, upper = None, None
        for x in range(bx):
            rho, p = rho_v[x, at, :], p_v[x, at, :]
            vel = [vel_v[k, x, at, :] for k in range(3)]
            side = (rho, vel, p, code_v[x, at, :].astype(f32) * (1.0 / 16.0), sound(rho, p))
            through = face(side, shifted(side, bz - 1, 1), 2, lane)
            total = [q - pltpu.roll(q, 1, 1) for q in through]
            if before is not None:
                across = face(before, side, 0)
                for k in range(5):
                    acc[k, x - 1, at, :] = upper[k] + across[k]
                total = [total[k] - across[k] for k in range(5)]
            before, upper = side, total
        for k in range(5):
            acc[k, bx - 1, at, :] = upper[k]
        return carry

    lax.fori_loop(0, by // high, inner, 0)

    halves = bz // 128

    def inner_y(i, carry):
        x = i // halves
        at = pl.ds(pl.multiple_of((i % halves) * 128, 128), 128)
        below = lax.broadcasted_iota(jnp.int32, (by, 128), 0) < by - 1
        rho, p = rho_v[x, :, at], p_v[x, :, at]
        vel = [vel_v[k, x, :, at] for k in range(3)]
        side = (rho, vel, p, code_v[x, :, at].astype(f32) * (1.0 / 16.0), sound(rho, p))
        through = face(side, shifted(side, by - 1, 0), 1, below)
        for k in range(5):
            acc[k, x, :, at] += through[k] - pltpu.roll(through[k], 1, 0)
        return carry

    lax.fori_loop(0, bx * halves, inner_y, 0)

    def packed(ref, slot):
        rho, p = ref[slot, 0], ref[slot, 4]
        return (rho, [ref[slot, 1 + k] for k in range(3)], p, ref[slot, 5], sound(rho, p))

    @pl.when(has_left)
    def _():
        edge_copy(1, 0, c - 1).wait_recv()
        through = face(packed(edge_in, 0), packed(edge_out, 0), 1)
        for k in range(5):
            for x in range(bx):
                acc[k, x, 0:1, :] -= through[k][x : x + 1]

    @pl.when(has_right)
    def _():
        edge_copy(0, 1, c + 1).wait_recv()
        through = face(packed(edge_out, 1), packed(edge_in, 1), 1)
        for k in range(5):
            for x in range(bx):
                acc[k, x, by - 1 : by, :] += through[k][x : x + 1]

    for step in range(1, cols):
        load_copy(step).wait_recv()
    total = loads[0]
    for other in range(1, cols):
        total = total + loads[other]
    keep = 1.0 - removed_v[...].astype(f32)
    start = rows_of([motion_v[k] for k in range(3)], 8)
    moved = (start + struct_step * total / mass_v[...]) * keep
    new_full[...] = moved
    own = new_full[:, pl.ds(pl.multiple_of(c * share, share), share)]
    for k in range(3):
        new_own[k] = own[k : k + 1]
    new_copy = pltpu.make_async_copy(new_own, new_h, new_sem)
    new_copy.start()
    moved = jnp.concatenate(parts_of(moved, 3) + [jnp.zeros_like(moved)], axis=0).astype(bf16)
    found = dot_nn(moved, at_elem)
    found = found[0:8] + found[8:16] + found[16:24]
    work = jnp.sum(rows_of(normals, 8) * found, axis=0, keepdims=True)
    source[3:4] = spread([weight * work])

    def join(i, carry):
        x = i // (by // high)
        at = pl.ds(pl.multiple_of((i % (by // high)) * high, high), high)
        rho, p = rho_v[x, at, :], p_v[x, at, :]
        state = conserved(rho, [vel_v[k, x, at, :] for k in range(3)], p)
        scale = step_ratio / (code_v[x, at, :].astype(f32) * (1.0 / 16.0))
        acc[0, x, at, :] = state[0] - scale * acc[0, x, at, :]
        for k in range(4):
            acc[1 + k, x, at, :] = state[1 + k] - scale * (
                acc[1 + k, x, at, :] - source[k, x, at, :]
            )
        return carry

    lax.fori_loop(0, bx * (by // high), join, 0)

    def out_copy(slot, piece):
        plane, at = slot * (bx - 1), pl.ds(piece * tall, tall)
        return pltpu.make_async_copy(
            acc.at[:, plane, at], out_h.at[:, plane, at], out_sem.at[slot, piece]
        )

    for slot in (1 - far, far):
        plane = slot * (bx - 1)
        sign = (1 - 2 * slot).astype(f32)

        for piece in range(pieces):

            @pl.when(has_way(slot))
            def _():
                for copy in plane_copies(1 - slot, piece, s - 1 + 2 * slot):
                    copy.wait_recv()

            def outer(i, carry):
                at = pl.ds(pl.multiple_of(piece * tall + i * high, high), high)
                rho, p = rho_v[plane, at, :], p_v[plane, at, :]
                vel = [vel_v[k, plane, at, :] for k in range(3)]
                own_fraction = code_v[plane, at, :].astype(f32) * (1.0 / 16.0)
                state = conserved(rho, vel, p)
                terms = flux(state, vel, p, 0)
                rho_n, p_n = halo_rho[slot, at, :], halo_p[slot, at, :]
                vel_n = [halo_vel[slot, k, at, :] for k in range(3)]
                fraction_n = halo_code[slot, at, :].astype(f32) * (1.0 / 16.0)
                state_n = conserved(rho_n, vel_n, p_n)
                terms_n = flux(state_n, vel_n, p_n, 0)
                speed = jnp.maximum(
                    jnp.abs(vel[0]) + sound(rho, p), jnp.abs(vel_n[0]) + sound(rho_n, p_n)
                )
                scale = (0.5 * step_ratio) * jnp.minimum(own_fraction, fraction_n) / own_fraction
                for k in range(5):
                    acc[k, plane, at, :] += scale * (
                        sign * (terms[k] + terms_n[k]) - speed * (state[k] - state_n[k])
                    )
                return carry

            lax.fori_loop(0, tall // high, outer, 0)
            out_copy(slot, piece).start()

    for slot in range(2):
        for piece in range(pieces):
            out_copy(slot, piece).wait()
    new_copy.wait()

    for way in range(2):

        @pl.when(has_way(way))
        def _():
            for piece in range(pieces):
                for copy in plane_copies(way, piece, s - 1 + 2 * way):
                    copy.wait_send()

    @pl.when(has_left)
    def _():
        edge_copy(0, 1, c - 1).wait_send()

    @pl.when(has_right)
    def _():
        edge_copy(1, 0, c + 1).wait_send()

    for step in range(1, cols):
        load_copy(step).wait_send()


def place_kernel(state, new, state_out, new_out, sem):
    copies = [
        pltpu.make_async_copy(state, state_out, sem.at[0]),
        pltpu.make_async_copy(new, new_out, sem.at[1]),
    ]
    for copy in copies:
        copy.start()
    for copy in copies:
        copy.wait()


def place(state, new):
    return pl.pallas_call(
        place_kernel,
        out_shape=tuple(jax.ShapeDtypeStruct(a.shape, a.dtype) for a in (state, new)),
        in_specs=[pl.BlockSpec(memory_space=pl.ANY)] * 2,
        out_specs=(pl.BlockSpec(memory_space=pl.ANY),) * 2,
        scratch_shapes=[pltpu.SemaphoreType.DMA((2,))],
        compiler_params=pltpu.CompilerParams(vmem_limit_bytes=4 * 1024 * 1024),
        name="place_results",
    )(state, new)


def local(slabs, cols, *args):
    density, velocity, pressure, code, cell, elem, count, normal, mass, removed, motion = args
    bx, by, bz = density.shape
    group = mass.shape[-1]
    share = group // cols
    plane = (by, bz)
    i32 = jnp.int32
    vmem, dma = pltpu.VMEM, pltpu.SemaphoreType.DMA
    args = [pltpu.with_memory_space_constraint(a, pltpu.HBM) if a.size > 1 else a for a in args]
    return place(*pl.pallas_call(
        functools.partial(step_kernel, slabs, cols),
        out_shape=(
            jax.ShapeDtypeStruct((5,) + density.shape, f32),
            jax.ShapeDtypeStruct((3, 1, share), f32),
        ),
        in_specs=[pl.BlockSpec(memory_space=pltpu.HBM)] * len(args),
        out_specs=(pl.BlockSpec(memory_space=pl.ANY), pl.BlockSpec(memory_space=pl.ANY)),
        scratch_shapes=[vmem(a.shape, a.dtype) for a in args]
        + [
            vmem((2,) + plane, f32),
            vmem((2, 3) + plane, f32),
            vmem((2,) + plane, f32),
            vmem((2,) + plane, i32),
            vmem((2, 6, bx, bz), f32),
            vmem((2, 6, bx, bz), f32),
            vmem((cols, 8, group), f32),
            vmem((4,) + density.shape, f32),
            vmem((5,) + density.shape, f32),
            vmem((8, group), f32),
            vmem((3, 1, share), f32),
            dma((len(args),)),
            dma((2, pieces, 4)),
            dma((2, pieces, 4)),
            dma((2,)),
            dma((2,)),
            dma((max(cols - 1, 1),)),
            dma((max(cols - 1, 1),)),
            dma((2, pieces)),
            dma,
        ],
        compiler_params=pltpu.CompilerParams(
            collective_id=0, has_side_effects=True, vmem_limit_bytes=16 * 1024 * 1024
        ),
        name="coupling_step",
    )(*args))


def solution(mesh):
    slabs, cols = mesh.shape["slab"], mesh.shape["col"]
    placed = (
        P("slab", "col", None),
        P(None, "slab", "col", None),
        P("slab", "col", None),
        P("slab", "col", None),
        P("slab", "col", None),
        P("slab", "col", None),
        P("slab", "col"),
        P(None, "slab", "col", None),
        P("slab", None),
        P("slab", None),
        P(None, "slab", None),
    )
    return jax.shard_map(
        functools.partial(local, slabs, cols),
        mesh=mesh,
        in_specs=placed,
        out_specs=(P(None, "slab", "col", None), P(None, "slab", "col")),
        check_vma=False,
    )
```

```python
import functools

import jax
import jax.numpy as jnp
from jax import lax
from jax.experimental import pallas as pl
from jax.experimental.pallas import tpu as pltpu
from jax.sharding import PartitionSpec as P

ratio_heat = 1.4
step_ratio = 0.1
struct_step = 1.0
pieces = 2

MESH = pl.DeviceIdType.MESH
f32 = jnp.float32
bf16 = jnp.bfloat16


def conserved(rho, vel, p):
    u, v, w = vel
    energy = p * (1.0 / (ratio_heat - 1.0)) + 0.5 * rho * (u * u + v * v + w * w)
    return [rho, rho * u, rho * v, rho * w, energy]


def flux(state, vel, p, along):
    normal = vel[along]
    terms = [normal * q for q in state]
    terms[1 + along] = terms[1 + along] + p
    terms[4] = terms[4] + p * normal
    return terms


def sound(rho, p):
    return jnp.sqrt(ratio_heat * p / rho)


def face(low, high, along, keep=None):
    rho_l, vel_l, p_l, f_l, c_l = low
    rho_h, vel_h, p_h, f_h, c_h = high
    state_l, state_h = conserved(rho_l, vel_l, p_l), conserved(rho_h, vel_h, p_h)
    flux_l, flux_h = flux(state_l, vel_l, p_l, along), flux(state_h, vel_h, p_h, along)
    speed = jnp.maximum(jnp.abs(vel_l[along]) + c_l, jnp.abs(vel_h[along]) + c_h)
    aperture = 0.5 * jnp.minimum(f_l, f_h)
    if keep is not None:
        aperture = jnp.where(keep, aperture, 0.0)
    return [
        aperture * ((flux_l[k] + flux_h[k]) - speed * (state_h[k] - state_l[k]))
        for k in range(5)
    ]


def shifted(side, amount, axis):
    rho, vel, p, f, c = side
    move = lambda a: pltpu.roll(a, amount, axis)
    return (move(rho), [move(v) for v in vel], move(p), move(f), move(c))


def parts_of(value, count):
    found = []
    for _ in range(count):
        head = value.astype(bf16).astype(f32)
        found.append(head)
        value = value - head
    return found


def rows_of(rows, height):
    width = rows[0].shape[-1]
    at = lax.broadcasted_iota(jnp.int32, (height, width), 0)
    total = jnp.zeros((height, width), f32)
    for k, row in enumerate(rows):
        total = jnp.where(at == k, row, total)
    return total


def dot_nn(a, b):
    return lax.dot_general(a, b, (((1,), (0,)), ((), ())), preferred_element_type=f32)


def dot_nt(a, b):
    return lax.dot_general(a, b, (((1,), (1,)), ((), ())), preferred_element_type=f32)


def step_kernel(
    slabs,
    cols,
    rho_h,
    vel_h,
    p_h,
    code_h,
    cell_h,
    elem_h,
    count_h,
    normal_h,
    mass_h,
    removed_h,
    motion_h,
    acc,
    new_own,
    rho_v,
    vel_v,
    p_v,
    code_v,
    cell_v,
    elem_v,
    count_v,
    normal_v,
    mass_v,
    removed_v,
    motion_v,
    halo_rho,
    halo_vel,
    halo_p,
    halo_code,
    edge_out,
    edge_in,
    loads,
    source,
    new_full,
    local_sem,
    x_send,
    x_recv,
    y_send,
    y_recv,
    l_send,
    l_recv,
):
    bx, by, bz = rho_v.shape
    rows = cell_v.shape[-1]
    group = mass_v.shape[-1]
    share = group // cols
    s, c = lax.axis_index("slab"), lax.axis_index("col")
    has_down, has_up = s > 0, s < slabs - 1
    has_left, has_right = c > 0, c < cols - 1

    pairs = [
        (p_h, p_v),
        (code_h, code_v),
        (cell_h, cell_v),
        (rho_h, rho_v),
        (vel_h, vel_v),
        (normal_h, normal_v),
        (elem_h, elem_v),
        (count_h, count_v),
        (mass_h, mass_v),
        (removed_h, removed_v),
        (motion_h, motion_v),
    ]
    fetches = [
        pltpu.make_async_copy(src, dst, local_sem.at[i]) for i, (src, dst) in enumerate(pairs)
    ]
    barrier = pltpu.get_barrier_semaphore()

    @pl.when(has_down)
    def _():
        pl.semaphore_signal(barrier, inc=1, device_id={"slab": s - 1}, device_id_type=MESH)

    @pl.when(has_up)
    def _():
        pl.semaphore_signal(barrier, inc=1, device_id={"slab": s + 1}, device_id_type=MESH)

    for step in range(1, cols):
        pl.semaphore_signal(
            barrier, inc=1, device_id={"col": lax.rem(c + step, cols)}, device_id_type=MESH
        )
    for fetch in fetches:
        fetch.start()
    pl.semaphore_wait(
        barrier, has_down.astype(jnp.int32) + has_up.astype(jnp.int32) + (cols - 1)
    )

    tall = by // pieces

    def plane_copies(way, piece, peer):
        plane, slot, at = way * (bx - 1), 1 - way, pl.ds(piece * tall, tall)
        return [
            pltpu.make_async_remote_copy(
                src_ref=src,
                dst_ref=dst,
                send_sem=x_send.at[way, piece, i],
                recv_sem=x_recv.at[slot, piece, i],
                device_id={"slab": peer},
                device_id_type=MESH,
            )
            for i, (src, dst) in enumerate(
                [
                    (vel_h.at[:, plane, at], halo_vel.at[slot, :, at]),
                    (rho_h.at[plane, at], halo_rho.at[slot, at]),
                    (p_h.at[plane, at], halo_p.at[slot, at]),
                    (code_h.at[plane, at], halo_code.at[slot, at]),
                ]
            )
        ]

    def has_way(way):
        return jnp.logical_and(s - 1 + 2 * way >= 0, s - 1 + 2 * way < slabs)

    def send_planes(way):
        @pl.when(has_way(way))
        def _():
            for piece in range(pieces):
                for copy in plane_copies(way, piece, s - 1 + 2 * way):
                    copy.start()

    far = lax.rem(s, 2)
    send_planes(far)

    def blank(slot):
        halo_rho[slot] = jnp.ones((by, bz), f32)
        halo_p[slot] = jnp.ones((by, bz), f32)
        halo_vel[slot] = jnp.zeros((3, by, bz), f32)
        halo_code[slot] = jnp.zeros((by, bz), jnp.int32)

    @pl.when(jnp.logical_not(has_down))
    def _():
        blank(0)

    @pl.when(jnp.logical_not(has_up))
    def _():
        blank(1)

    for fetch in fetches:
        fetch.wait()

    for side, y in ((0, 0), (1, by - 1)):
        for x in range(bx):
            edge_out[side, 0, x : x + 1, :] = rho_v[x, y : y + 1, :]
            for k in range(3):
                edge_out[side, 1 + k, x : x + 1, :] = vel_v[k, x, y : y + 1, :]
            edge_out[side, 4, x : x + 1, :] = p_v[x, y : y + 1, :]
            edge_out[side, 5, x : x + 1, :] = code_v[x, y : y + 1, :].astype(f32) * (1.0 / 16.0)

    def edge_copy(side, slot, peer):
        return pltpu.make_async_remote_copy(
            src_ref=edge_out.at[side],
            dst_ref=edge_in.at[slot],
            send_sem=y_send.at[slot],
            recv_sem=y_recv.at[slot],
            device_id={"col": peer},
            device_id_type=MESH,
        )

    @pl.when(has_left)
    def _():
        edge_copy(0, 1, c - 1).start()

    @pl.when(has_right)
    def _():
        edge_copy(1, 0, c + 1).start()

    cells = cell_v[0]
    line = lax.shift_right_logical(cells, bz.bit_length() - 1)
    place = lax.bitwise_and(cells, bz - 1)
    at_line = lax.broadcasted_iota(jnp.int32, (bx * by, rows), 0) == line
    at_place = (lax.broadcasted_iota(jnp.int32, (bz, rows), 0) == place).astype(f32).astype(bf16)
    at_elem = (
        (lax.broadcasted_iota(jnp.int32, (group, rows), 0) == elem_v[0]).astype(f32).astype(bf16)
    )
    active = (lax.broadcasted_iota(jnp.int32, (1, rows), 1) < count_v[...]).astype(f32)

    fraction = code_v[...].astype(f32) * (1.0 / 16.0)
    wetted = (p_v[...] * (1.0 - fraction)).reshape(bx * by, bz)
    picked = dot_nn(jnp.concatenate(parts_of(wetted, 3), axis=0).astype(bf16), at_place)
    size = bx * by
    picked = picked[:size] + picked[size : 2 * size] + picked[2 * size :]
    weight = jnp.sum(jnp.where(at_line, picked, 0.0), axis=0, keepdims=True) * active
    normals = [normal_v[k, 0] for k in range(3)]
    pushes = [weight * n for n in normals]

    force = rows_of([-q for q in pushes], 8)
    force = jnp.concatenate(parts_of(force, 3) + [jnp.zeros_like(force)], axis=0).astype(bf16)
    found = dot_nt(force, at_elem)
    loads[c] = found[0:8] + found[8:16] + found[16:24]

    def load_copy(step):
        return pltpu.make_async_remote_copy(
            src_ref=loads.at[c],
            dst_ref=loads.at[c],
            send_sem=l_send.at[step - 1],
            recv_sem=l_recv.at[step - 1],
            device_id={"col": lax.rem(c + step, cols)},
            device_id_type=MESH,
        )

    for step in range(1, cols):
        load_copy(step).start()
    send_planes(1 - far)

    def spread(values):
        total = None
        for part in zip(*[parts_of(v, 2) for v in values]):
            lhs = jnp.concatenate([jnp.where(at_line, q, 0.0) for q in part], axis=0)
            found = dot_nt(lhs.astype(bf16), at_place)
            total = found if total is None else total + found
        return total.reshape(len(values), bx, by, bz)

    source[0:3] = spread(pushes)

    high = 16

    def inner(i, carry):
        at = pl.ds(pl.multiple_of(i * high, high), high)
        lane = lax.broadcasted_iota(jnp.int32, (high, bz), 1) < bz - 1
        before, upper = None, None
        for x in range(bx):
            rho, p = rho_v[x, at, :], p_v[x, at, :]
            vel = [vel_v[k, x, at, :] for k in range(3)]
            side = (rho, vel, p, code_v[x, at, :].astype(f32) * (1.0 / 16.0), sound(rho, p))
            through = face(side, shifted(side, bz - 1, 1), 2, lane)
            total = [q - pltpu.roll(q, 1, 1) for q in through]
            if before is not None:
                across = face(before, side, 0)
                for k in range(5):
                    acc[k, x - 1, at, :] = upper[k] + across[k]
                total = [total[k] - across[k] for k in range(5)]
            before, upper = side, total
        for k in range(5):
            acc[k, bx - 1, at, :] = upper[k]
        return carry

    lax.fori_loop(0, by // high, inner, 0)

    halves = bz // 128

    def inner_y(i, carry):
        x = i // halves
        at = pl.ds(pl.multiple_of((i % halves) * 128, 128), 128)
        below = lax.broadcasted_iota(jnp.int32, (by, 128), 0) < by - 1
        rho, p = rho_v[x, :, at], p_v[x, :, at]
        vel = [vel_v[k, x, :, at] for k in range(3)]
        side = (rho, vel, p, code_v[x, :, at].astype(f32) * (1.0 / 16.0), sound(rho, p))
        through = face(side, shifted(side, by - 1, 0), 1, below)
        for k in range(5):
            acc[k, x, :, at] += through[k] - pltpu.roll(through[k], 1, 0)
        return carry

    lax.fori_loop(0, bx * halves, inner_y, 0)

    def packed(ref, slot):
        rho, p = ref[slot, 0], ref[slot, 4]
        return (rho, [ref[slot, 1 + k] for k in range(3)], p, ref[slot, 5], sound(rho, p))

    @pl.when(has_left)
    def _():
        edge_copy(1, 0, c - 1).wait_recv()
        through = face(packed(edge_in, 0), packed(edge_out, 0), 1)
        for k in range(5):
            for x in range(bx):
                acc[k, x, 0:1, :] -= through[k][x : x + 1]

    @pl.when(has_right)
    def _():
        edge_copy(0, 1, c + 1).wait_recv()
        through = face(packed(edge_out, 1), packed(edge_in, 1), 1)
        for k in range(5):
            for x in range(bx):
                acc[k, x, by - 1 : by, :] += through[k][x : x + 1]

    for step in range(1, cols):
        load_copy(step).wait_recv()
    total = loads[0]
    for other in range(1, cols):
        total = total + loads[other]
    keep = 1.0 - removed_v[...].astype(f32)
    start = rows_of([motion_v[k] for k in range(3)], 8)
    moved = (start + struct_step * total / mass_v[...]) * keep
    new_full[...] = moved
    own = new_full[:, pl.ds(pl.multiple_of(c * share, share), share)]
    for k in range(3):
        new_own[k] = own[k : k + 1]
    moved = jnp.concatenate(parts_of(moved, 3) + [jnp.zeros_like(moved)], axis=0).astype(bf16)
    found = dot_nn(moved, at_elem)
    found = found[0:8] + found[8:16] + found[16:24]
    work = jnp.sum(rows_of(normals, 8) * found, axis=0, keepdims=True)
    source[3:4] = spread([weight * work])

    def join(i, carry):
        x = i // (by // high)
        at = pl.ds(pl.multiple_of((i % (by // high)) * high, high), high)
        rho, p = rho_v[x, at, :], p_v[x, at, :]
        state = conserved(rho, [vel_v[k, x, at, :] for k in range(3)], p)
        scale = step_ratio / (code_v[x, at, :].astype(f32) * (1.0 / 16.0))
        acc[0, x, at, :] = state[0] - scale * acc[0, x, at, :]
        for k in range(4):
            acc[1 + k, x, at, :] = state[1 + k] - scale * (
                acc[1 + k, x, at, :] - source[k, x, at, :]
            )
        return carry

    lax.fori_loop(0, bx * (by // high), join, 0)

    for slot in (1 - far, far):
        plane = slot * (bx - 1)
        sign = (1 - 2 * slot).astype(f32)

        for piece in range(pieces):

            @pl.when(has_way(slot))
            def _():
                for copy in plane_copies(1 - slot, piece, s - 1 + 2 * slot):
                    copy.wait_recv()

            def outer(i, carry):
                at = pl.ds(pl.multiple_of(piece * tall + i * high, high), high)
                rho, p = rho_v[plane, at, :], p_v[plane, at, :]
                vel = [vel_v[k, plane, at, :] for k in range(3)]
                own_fraction = code_v[plane, at, :].astype(f32) * (1.0 / 16.0)
                state = conserved(rho, vel, p)
                terms = flux(state, vel, p, 0)
                rho_n, p_n = halo_rho[slot, at, :], halo_p[slot, at, :]
                vel_n = [halo_vel[slot, k, at, :] for k in range(3)]
                fraction_n = halo_code[slot, at, :].astype(f32) * (1.0 / 16.0)
                state_n = conserved(rho_n, vel_n, p_n)
                terms_n = flux(state_n, vel_n, p_n, 0)
                speed = jnp.maximum(
                    jnp.abs(vel[0]) + sound(rho, p), jnp.abs(vel_n[0]) + sound(rho_n, p_n)
                )
                scale = (0.5 * step_ratio) * jnp.minimum(own_fraction, fraction_n) / own_fraction
                for k in range(5):
                    acc[k, plane, at, :] += scale * (
                        sign * (terms[k] + terms_n[k]) - speed * (state[k] - state_n[k])
                    )
                return carry

            lax.fori_loop(0, tall // high, outer, 0)

    for way in range(2):

        @pl.when(has_way(way))
        def _():
            for piece in range(pieces):
                for copy in plane_copies(way, piece, s - 1 + 2 * way):
                    copy.wait_send()

    @pl.when(has_left)
    def _():
        edge_copy(0, 1, c - 1).wait_send()

    @pl.when(has_right)
    def _():
        edge_copy(1, 0, c + 1).wait_send()

    for step in range(1, cols):
        load_copy(step).wait_send()


def place_kernel(state, new, state_out, new_out, sem):
    copies = [
        pltpu.make_async_copy(state, state_out, sem.at[0]),
        pltpu.make_async_copy(new, new_out, sem.at[1]),
    ]
    for copy in copies:
        copy.start()
    for copy in copies:
        copy.wait()


def place(state, new):
    return pl.pallas_call(
        place_kernel,
        out_shape=tuple(jax.ShapeDtypeStruct(a.shape, a.dtype) for a in (state, new)),
        in_specs=[pl.BlockSpec(memory_space=pl.ANY)] * 2,
        out_specs=(pl.BlockSpec(memory_space=pl.ANY),) * 2,
        scratch_shapes=[pltpu.SemaphoreType.DMA((2,))],
        compiler_params=pltpu.CompilerParams(vmem_limit_bytes=4 * 1024 * 1024),
        name="place_results",
    )(state, new)


def local(slabs, cols, *args):
    density, velocity, pressure, code, cell, elem, count, normal, mass, removed, motion = args
    bx, by, bz = density.shape
    group = mass.shape[-1]
    share = group // cols
    plane = (by, bz)
    i32 = jnp.int32
    vmem, dma = pltpu.VMEM, pltpu.SemaphoreType.DMA
    args = [pltpu.with_memory_space_constraint(a, pltpu.HBM) if a.size > 1 else a for a in args]
    return place(*pl.pallas_call(
        functools.partial(step_kernel, slabs, cols),
        out_shape=(
            jax.ShapeDtypeStruct((5,) + density.shape, f32),
            jax.ShapeDtypeStruct((3, 1, share), f32),
        ),
        in_specs=[pl.BlockSpec(memory_space=pltpu.HBM)] * len(args),
        out_specs=(pl.BlockSpec(memory_space=pltpu.VMEM), pl.BlockSpec(memory_space=pltpu.VMEM)),
        scratch_shapes=[vmem(a.shape, a.dtype) for a in args]
        + [
            vmem((2,) + plane, f32),
            vmem((2, 3) + plane, f32),
            vmem((2,) + plane, f32),
            vmem((2,) + plane, i32),
            vmem((2, 6, bx, bz), f32),
            vmem((2, 6, bx, bz), f32),
            vmem((cols, 8, group), f32),
            vmem((4,) + density.shape, f32),
            vmem((8, group), f32),
            dma((len(args),)),
            dma((2, pieces, 4)),
            dma((2, pieces, 4)),
            dma((2,)),
            dma((2,)),
            dma((max(cols - 1, 1),)),
            dma((max(cols - 1, 1),)),
        ],
        compiler_params=pltpu.CompilerParams(
            collective_id=0, has_side_effects=True, vmem_limit_bytes=16 * 1024 * 1024
        ),
        name="coupling_step",
    )(*args))


def solution(mesh):
    slabs, cols = mesh.shape["slab"], mesh.shape["col"]
    placed = (
        P("slab", "col", None),
        P(None, "slab", "col", None),
        P("slab", "col", None),
        P("slab", "col", None),
        P("slab", "col", None),
        P("slab", "col", None),
        P("slab", "col"),
        P(None, "slab", "col", None),
        P("slab", None),
        P("slab", None),
        P(None, "slab", None),
    )
    return jax.shard_map(
        functools.partial(local, slabs, cols),
        mesh=mesh,
        in_specs=placed,
        out_specs=(P(None, "slab", "col", None), P(None, "slab", "col")),
        check_vma=False,
    )
```
